256 devices in a mesh: leaf: 64 (over x, z, core), blk: 4 (over y).
Axes of the slice: x: 4, y: 4, z: 8, core: 2. Of those that a mesh axis runs over, the one named last changes fastest.
Arguments:
- features: float32 [64, 262144], P(None, ('leaf', 'blk')), may hold values from -6 to 6
- sketch: float32 [256, 262144], P(None, ('leaf', 'blk')), may hold values from -12 to 12
- omega: float32 [256, 262144], P(None, ('leaf', 'blk')), may hold values from -6 to 6
- slot: int32 [262144], P(('leaf', 'blk')), may hold values from 0 to 262143, as said below
- column_order: int32 [6, 256], replicated, may hold values from 0 to 255, each once within a row
Outputs:
- leaf_basis: float32 [256, 262144], P(None, ('leaf', 'blk'))
- transfers: float32 [64, 6, 512, 256], P('leaf')
The draws below stay inside these ranges and needn't reach their ends.
Inputs may be any that keep to these rules, and one draw needn't show every extreme that they name: slot is a permutation of all points; a point goes to a device with the same blk index as its own, and every device sends exactly 1024 // 64 of its points to each leaf index.
All inputs are finite; a program needn't handle non-finite values.
Results may differ from the reference program's by a relative error of at most 0.0003.
Values sent between devices are 32-bit elements; how exact they have to be, the bound alone decides.
A program may use at most 128 MiB of HBM per device.

```python
import math
import jax
import jax.numpy as jnp
from jax import lax

F = 64
R = 256
P_DEV = 1024
LEAF = 4096
N = 262144
LEVELS = 6
N_LEAF = 64
N_BLK = 4


def draw_slot(key, part):
    key = jax.random.fold_in(key, 11)
    per_peer = P_DEV // N_LEAF
    key_target, key_place = jax.random.split(key)
    ordered = jnp.broadcast_to(jnp.arange(P_DEV, dtype=jnp.int32), (N_BLK, N_LEAF, P_DEV))
    shuffle = jax.random.permutation(key_target, ordered, axis=2, independent=True)
    placing = jax.random.permutation(key_place, ordered, axis=2, independent=True)
    target = shuffle // per_peer
    arrival = jnp.arange(N_LEAF, dtype=jnp.int32)[None, :, None] * per_peer + shuffle % per_peer
    blocks = jnp.arange(N_BLK, dtype=jnp.int32)[:, None, None]
    position = placing[blocks, target, arrival]
    slot_values = (target * N_BLK + blocks) * P_DEV + position
    return jnp.transpose(slot_values, (1, 0, 2)).reshape(N).astype(jnp.int32)


def level_of(stream_key, extent, pieces, low, largest):
    def one(axis_at, parts):
        draws = jax.random.uniform(jax.random.fold_in(jax.random.fold_in(stream_key, 6), axis_at), (parts,), jnp.float32, low / len(pieces), largest / len(pieces))
        return jnp.repeat(jnp.exp(draws), extent[axis_at] // parts).reshape((-1,) + (1,) * (len(extent) - axis_at - 1))

    factor_of = one(*pieces[0])
    for cut in pieces[1:]:
        factor_of = factor_of * one(*cut)
    return factor_of


def bell_draw(stream_key, extent, scale, limit, shards=(), held_as=jnp.bfloat16):
    result = jax.random.normal(stream_key, extent, jnp.float32) * scale
    if len(shards) > 0:
        result = level_of(stream_key, extent, shards, -0.22, 0.18) * result
    return jnp.clip(result, min=-limit, max=limit).astype(held_as)


def setup_inputs(seed: int = 0) -> dict:
    splits = jax.random.split(jax.random.key(seed), 6)
    features = bell_draw(splits[0], (F, N), 1.0, 6.0, ((1, 256),), jnp.float32)
    sketch = bell_draw(splits[1], (R, N), 2.0, 12.0, ((1, 256),), jnp.float32)
    omega = bell_draw(splits[2], (R, N), 1.0, 6.0, ((1, 256),), jnp.float32)
    slot = draw_slot(jax.random.fold_in(splits[5], 71), 0)
    column_order = jax.vmap(lambda own: jax.random.permutation(own, R))(jax.random.split(splits[4], LEVELS)).reshape((LEVELS, R)).astype(jnp.int32)
    return dict(features=features, sketch=sketch, omega=omega, slot=slot, column_order=column_order)


def kernel_block(row_feat, col_feat):
    width = row_feat.shape[0]
    inner = lax.dot_general(row_feat.astype(jnp.float32), col_feat.astype(jnp.float32), (((0,), (0,)), ((), ())), precision=lax.Precision.HIGHEST, preferred_element_type=jnp.float32)
    norms_a = lax.optimization_barrier(jnp.sum(row_feat * row_feat, axis=0))
    norms_b = lax.optimization_barrier(jnp.sum(col_feat * col_feat, axis=0))
    distance = norms_a[:, None] + norms_b[None, :] - 2.0 * inner
    return jnp.exp(distance * (-2.0 / width))

def reference(features, sketch, omega, slot, column_order):
    tree_feat = jnp.zeros_like(features).at[:, slot].set(features)
    tree_sketch = jnp.zeros_like(sketch).at[:, slot].set(sketch)
    tree_omega = jnp.zeros_like(omega).at[:, slot].set(omega)

    def one_leaf(leaf_id):
        begin = leaf_id * LEAF
        columns = lax.dynamic_slice_in_dim(tree_feat, begin, LEAF, 1)
        sketch_cols = lax.dynamic_slice_in_dim(tree_sketch, begin, LEAF, 1)
        omega_cols = lax.dynamic_slice_in_dim(tree_omega, begin, LEAF, 1)
        kernel = kernel_block(columns, columns)
        near_field = jnp.dot(omega_cols.astype(jnp.float32), kernel.astype(jnp.float32), precision=lax.Precision.HIGHEST, preferred_element_type=jnp.float32)
        off_sketch = sketch_cols - near_field
        gram = lax.dot_general(off_sketch.astype(jnp.float32), off_sketch.astype(jnp.float32), (((1,), (1,)), ((), ())), precision=lax.Precision.HIGHEST, preferred_element_type=jnp.float32)
        lower = jnp.linalg.cholesky(gram)
        basis_t = lax.linalg.triangular_solve(lower, off_sketch, left_side=True, lower=True)
        return (basis_t * math.sqrt(LEAF), jnp.transpose(lower))
    bases, factors = lax.map(one_leaf, jnp.arange(N_LEAF, dtype=jnp.int32))
    leaf_basis = jnp.transpose(bases, (1, 0, 2)).reshape(R, N)

    def merge_one(stacked):
        gram = lax.dot_general(stacked.astype(jnp.float32), stacked.astype(jnp.float32), (((0,), (0,)), ((), ())), precision=lax.Precision.HIGHEST, preferred_element_type=jnp.float32)
        lower = jnp.linalg.cholesky(gram)
        ortho_t = lax.linalg.triangular_solve(lower, jnp.transpose(stacked), left_side=True, lower=True)
        return (jnp.transpose(ortho_t) * math.sqrt(2 * R), jnp.transpose(lower))
    collected = []
    for height in range(LEVELS):
        paired = factors.reshape(-1, 2 * R, R)
        paired = jnp.take(paired, column_order[height], axis=2)
        transfer, factors = jax.vmap(merge_one)(paired)
        collected.append(jnp.repeat(transfer, 2 ** (height + 1), axis=0))
    return (leaf_basis, jnp.stack(collected, axis=1))
```

```python
import functools
import math

import jax
import jax.numpy as jnp
from jax import lax
from jax.experimental import pallas as pl
from jax.experimental.pallas import tpu as pltpu
from jax.sharding import PartitionSpec as P

NN = (((1,), (0,)), ((), ()))
NT = (((1,), (1,)), ((), ()))
TN = (((0,), (0,)), ((), ()))
f32, bf16 = jnp.float32, jnp.bfloat16


def mm(a, b, dims):
    return lax.dot_general(a, b, dims, preferred_element_type=f32)


def halves(x):
    hi = x.astype(bf16)
    return hi, (x - hi.astype(f32)).astype(bf16)


def thirds(x):
    hi = x.astype(bf16)
    rest = x - hi.astype(f32)
    mid = rest.astype(bf16)
    return hi, mid, (rest - mid.astype(f32)).astype(bf16)


def dot3(a, b, dims):
    return mm(a[0], b[0], dims) + (mm(a[0], b[1], dims) + mm(a[1], b[0], dims))


def dotf(a, b, dims):
    return dot3(halves(a), halves(b), dims)


def pick(x, hot, dims, left):
    parts = thirds(x)
    if left:
        return mm(parts[0], hot, dims) + mm(parts[1], hot, dims) + mm(parts[2], hot, dims)
    return mm(hot, parts[0], dims) + mm(hot, parts[1], dims) + mm(hot, parts[2], dims)


NB = 32
W = 8


def row_of(x, k):
    return jnp.broadcast_to(x[k:k + 1, :], x.shape)


def diag_inverse(a, seg_base, rows):
    lane = lax.broadcasted_iota(jnp.int32, (NB, 128), 1)
    b = jnp.where(lane - seg_base == rows, 1.0, 0.0).astype(f32)
    scale = jnp.zeros((NB, 128), f32)
    for k0 in range(0, NB, W):
        cols = [jnp.take_along_axis(a, seg_base + (k0 + i), axis=1, mode="promise_in_bounds") for i in range(W)]
        ra = [row_of(a, k0 + i) for i in range(W)]
        rb = [row_of(b, k0 + i) for i in range(W)]
        mult = []
        for i in range(W):
            k = k0 + i
            pivot = row_of(cols[i], k)
            root = lax.rsqrt(pivot)
            scale = jnp.where(rows == k, root, scale)
            m = jnp.where(rows > k, cols[i] * (root * root), 0.0)
            mult.append(m)
            for t in range(i + 1, W):
                cols[t] = cols[t] - m * row_of(cols[t], k)
                mt = row_of(m, k0 + t)
                ra[t] = ra[t] - mt * ra[i]
                rb[t] = rb[t] - mt * rb[i]
        for i in range(W):
            if k0 + W < NB:
                a = a - mult[i] * ra[i]
            b = b - mult[i] * rb[i]
    return b * scale


def tri_kernel(n_inv_groups, order_ref, gram_ref, second_ref, rhs_ref, basis_ref, trans_ref,
               own, sib, panel, inv, fact, finv):
    groups = 4
    size = gram_ref.shape[1]
    steps = size // NB
    depth = order_ref.shape[0]
    slots = 2 * depth + 1
    isub = lax.broadcasted_iota(jnp.int32, (size, size), 0)
    hot = [jnp.where(isub == order_ref[l:l + 1, :], 1.0, 0.0).astype(bf16) for l in range(depth)]
    total = [hot[0]]
    for l in range(1, depth):
        total.append(mm(total[-1], hot[l], NN).astype(bf16))

    def reorder(g, q):
        return pick(pick(g, q, NN, True), q, TN, False)

    running = gram_ref[0]
    own[0] = running
    for l in range(depth):
        g = gram_ref[l + 1]
        sib[l] = g if l == 0 else reorder(g, total[l - 1])
        running = running + g
        own[l + 1] = reorder(running, total[l])

    def dense(s):
        if s <= depth:
            return own, s
        return sib, min(s - depth - 1, depth - 1)

    for j in range(steps):
        for g in range(groups):
            lo = NB * j
            pieces = []
            for t in range(4):
                ref, at = dense(min(4 * g + t, slots - 1))
                pieces.append(ref[at, lo:lo + NB, :])
            panel[g, j] = jnp.concatenate(pieces, axis=0).T

    lane = lax.broadcasted_iota(jnp.int32, (NB, 128), 1)
    rows = lax.broadcasted_iota(jnp.int32, (NB, 128), 0)
    seg_base = (lane // NB) * NB
    r128 = lax.broadcasted_iota(jnp.int32, (128, 128), 0) // NB
    l128 = lax.broadcasted_iota(jnp.int32, (128, 128), 1) // NB
    same = r128 == l128

    def spread(x):
        return jnp.where(same, jnp.concatenate([x] * 4, axis=0), 0.0)

    for j in range(steps):
        lo = NB * j
        nxt = lo + NB
        for g in range(groups):
            d = panel[g, j, lo:nxt, :]
            li = diag_inverse(d, seg_base, rows)
            lp = dotf(panel[g, j, lo:, :], spread(li), NT)
            top = jnp.where(lane - seg_base <= rows, lp[:NB], 0.0)
            if lo:
                panel[g, j, :lo, :] = jnp.zeros((lo, 128), f32)
            panel[g, j, lo:nxt, :] = top
            if nxt < size:
                panel[g, j, nxt:, :] = lp[NB:]
                low = lp[NB:]
                lowh = halves(low)
                for i in range(j + 1, steps):
                    at = NB * (i - j - 1)
                    rhs = halves(spread(low[at:at + NB]))
                    panel[g, i, NB * i:, :] -= dot3((lowh[0][at:], lowh[1][at:]), rhs, NT)
            if g < n_inv_groups:
                lih = halves(li)
                for c in range(j + 1):
                    if c == j:
                        x = li
                    else:
                        x = dot3(lih, halves(spread(inv[g, c, lo:nxt, :])), NN)
                    inv[g, c, lo:nxt, :] = x
                    if nxt < size:
                        upd = dot3(lowh, halves(spread(x)), NN)
                        if c == j:
                            inv[g, c, nxt:, :] = -upd
                        else:
                            inv[g, c, nxt:, :] -= upd
                if lo:
                    inv[g, j, :lo, :] = jnp.zeros((lo, 128), f32)

    for j in range(steps):
        for g in range(groups):
            flat = panel[g, j].T
            for t in range(4):
                if 4 * g + t < slots:
                    fact[4 * g + t, NB * j:NB * j + NB, :] = flat[NB * t:NB * t + NB]
            if g < n_inv_groups:
                flat = inv[g, j].T
                for t in range(4):
                    if 4 * g + t <= depth:
                        finv[4 * g + t, NB * j:NB * j + NB, :] = flat[NB * t:NB * t + NB]

    basis_ref[...] = dotf(finv[0] * math.sqrt(4096), rhs_ref[...], TN)
    for l in range(depth):
        v = halves(pick(finv[l + 1] * math.sqrt(2 * size), hot[l], NN, False))
        second = second_ref[l]
        trans_ref[l, pl.ds(pl.multiple_of(second * size, size), size), :] = dot3(halves(fact[l]), v, NN)
        trans_ref[l, pl.ds(pl.multiple_of((1 - second) * size, size), size), :] = dot3(
            halves(fact[depth + 1 + l]), v, NN)


def tri(order, grams, second, rhs):
    depth, size = order.shape
    return pl.pallas_call(
        functools.partial(tri_kernel, 2),
        out_shape=(jax.ShapeDtypeStruct(rhs.shape, f32), jax.ShapeDtypeStruct((depth, 2 * size, size), f32)),
        in_specs=[pl.BlockSpec(memory_space=pltpu.VMEM), pl.BlockSpec(memory_space=pltpu.VMEM),
                  pl.BlockSpec(memory_space=pltpu.SMEM), pl.BlockSpec(memory_space=pltpu.VMEM)],
        out_specs=[pl.BlockSpec(memory_space=pltpu.VMEM)] * 2,
        scratch_shapes=[
            pltpu.VMEM((depth + 1, size, size), f32),
            pltpu.VMEM((depth, size, size), f32),
            pltpu.VMEM((4, 8, size, 128), f32),
            pltpu.VMEM((2, 8, size, 128), f32),
            pltpu.VMEM((2 * depth + 1, size, size), f32),
            pltpu.VMEM((depth + 1, size, size), f32),
        ],
        compiler_params=pltpu.CompilerParams(vmem_limit_bytes=48 << 20),
    )(order, grams, second, rhs)


def partner(block, axis, stride):
    count = lax.axis_size(axis)
    route = []
    for low in range(count):
        high = low | 1 << stride
        if high != low and high < count:
            route += [(low, high), (high, low)]
    return lax.ppermute(block, axis, route)


def kernel_block(row_feat, col_feat):
    width = row_feat.shape[0]
    inner = lax.dot_general(
        row_feat,
        col_feat,
        (((0,), (0,)), ((), ())),
        precision=lax.Precision.HIGHEST,
        preferred_element_type=jnp.float32,
    )
    norms_a = jnp.sum(row_feat * row_feat, axis=0)
    norms_b = jnp.sum(col_feat * col_feat, axis=0)
    distance = norms_a[:, None] + norms_b[None, :] - 2.0 * inner
    return jnp.exp(distance * (-2.0 / width))


def per_device(features, sketch, omega, slot, column_order):
    points = features.shape[1]
    rank = sketch.shape[0]
    blk_count = lax.axis_size("blk")
    leaf_count = lax.axis_size("leaf")
    sending = jnp.argsort(slot)
    sorted_slot = slot[sending]
    position_row = (sorted_slot % points).astype(jnp.float32)[None, :]
    received = (
        lax.all_to_all(features[:, sending], "leaf", split_axis=1, concat_axis=1, tiled=True),
        lax.all_to_all(sketch[:, sending], "leaf", split_axis=1, concat_axis=1, tiled=True),
        lax.all_to_all(omega[:, sending], "leaf", split_axis=1, concat_axis=1, tiled=True),
        lax.all_to_all(position_row, "leaf", split_axis=1, concat_axis=1, tiled=True),
    )
    arrived_pos = received[3][0].astype(jnp.int32)
    inverse = jnp.argsort(arrived_pos)
    tree_feat = received[0][:, inverse]
    tree_sketch = received[1][:, inverse]
    tree_omega = received[2][:, inverse]
    kernel = kernel_block(lax.all_gather(tree_feat, "blk", axis=1, tiled=True), tree_feat)
    near_field = jnp.dot(
        lax.all_gather(tree_omega, "blk", axis=1, tiled=True),
        kernel,
        precision=lax.Precision.HIGHEST,
        preferred_element_type=jnp.float32,
    )
    off_sketch = tree_sketch - near_field
    local_gram = lax.dot_general(
        off_sketch,
        off_sketch,
        (((1,), (1,)), ((), ())),
        precision=lax.Precision.HIGHEST,
        preferred_element_type=jnp.float32,
    )
    gram = lax.psum(local_gram, "blk")
    leaf_id = lax.axis_index("leaf")
    depth = column_order.shape[0]
    grams = [gram]
    running = gram
    for height in range(depth):
        grams.append(partner(running, "leaf", height))
        running = running + grams[-1]
    second = leaf_id >> jnp.arange(depth, dtype=jnp.int32) & 1
    leaf_basis, transfers = tri(column_order, jnp.stack(grams), second, off_sketch)
    return (leaf_basis, transfers[None])


def solution(mesh):
    placed = (
        P(None, ("leaf", "blk")),
        P(None, ("leaf", "blk")),
        P(None, ("leaf", "blk")),
        P(("leaf", "blk")),
        P(),
    )
    return jax.shard_map(
        per_device,
        mesh=mesh,
        in_specs=placed,
        out_specs=(P(None, ("leaf", "blk")), P("leaf", None, None, None)),
        check_vma=False,
    )
```

```python
import functools
import math

import jax
import jax.numpy as jnp
from jax import lax
from jax.experimental import pallas as pl
from jax.experimental.pallas import tpu as pltpu
from jax.sharding import PartitionSpec as P

NN = (((1,), (0,)), ((), ()))
NT = (((1,), (1,)), ((), ()))
TN = (((0,), (0,)), ((), ()))
f32, bf16 = jnp.float32, jnp.bfloat16


def mm(a, b, dims):
    return lax.dot_general(a, b, dims, preferred_element_type=f32)


def halves(x):
    hi = x.astype(bf16)
    return hi, (x - hi.astype(f32)).astype(bf16)


def thirds(x):
    hi = x.astype(bf16)
    rest = x - hi.astype(f32)
    mid = rest.astype(bf16)
    return hi, mid, (rest - mid.astype(f32)).astype(bf16)


def dot3(a, b, dims):
    return mm(a[0], b[0], dims) + (mm(a[0], b[1], dims) + mm(a[1], b[0], dims))


def dotf(a, b, dims):
    return dot3(halves(a), halves(b), dims)


def pick(x, hot, dims, left):
    parts = thirds(x)
    if left:
        return mm(parts[0], hot, dims) + mm(parts[1], hot, dims) + mm(parts[2], hot, dims)
    return mm(hot, parts[0], dims) + mm(hot, parts[1], dims) + mm(hot, parts[2], dims)


NB = 32
W = 8


def row_of(x, k):
    return jnp.broadcast_to(x[k:k + 1, :], x.shape)


def diag_inverse(a, seg_base, rows):
    lane = lax.broadcasted_iota(jnp.int32, (NB, 128), 1)
    b = jnp.where(lane - seg_base == rows, 1.0, 0.0).astype(f32)
    scale = jnp.zeros((NB, 128), f32)
    for k0 in range(0, NB, W):
        cols = [jnp.take_along_axis(a, seg_base + (k0 + i), axis=1, mode="promise_in_bounds") for i in range(W)]
        ra = [row_of(a, k0 + i) for i in range(W)]
        rb = [row_of(b, k0 + i) for i in range(W)]
        mult = []
        for i in range(W):
            k = k0 + i
            pivot = row_of(cols[i], k)
            root = lax.rsqrt(pivot)
            scale = jnp.where(rows == k, root, scale)
            m = jnp.where(rows > k, cols[i] * (root * root), 0.0)
            mult.append(m)
            for t in range(i + 1, W):
                cols[t] = cols[t] - m * row_of(cols[t], k)
                mt = row_of(m, k0 + t)
                ra[t] = ra[t] - mt * ra[i]
                rb[t] = rb[t] - mt * rb[i]
        for i in range(W):
            if k0 + W < NB:
                a = a - mult[i] * ra[i]
            b = b - mult[i] * rb[i]
    return b * scale


def tri_kernel(n_inv_groups, order_ref, gram_ref, second_ref, rhs_ref, basis_ref, trans_ref,
               own, sib, panel, inv, fact, finv):
    groups = 4
    size = order_ref.shape[1]
    half = size // 2
    steps = size // NB
    depth = order_ref.shape[0]
    slots = 2 * depth + 1
    isub = lax.broadcasted_iota(jnp.int32, (size, size), 0)
    hot = [jnp.where(isub == order_ref[l:l + 1, :], 1.0, 0.0).astype(bf16) for l in range(depth)]
    total = [hot[0]]
    for l in range(1, depth):
        total.append(mm(total[-1], hot[l], NN).astype(bf16))

    def reorder(g, q):
        return pick(pick(g, q, NN, True), q, TN, False)

    def unfold(at):
        low = gram_ref[at, half:2 * half, :]
        top = jnp.concatenate([gram_ref[at, 0:half, :], jnp.transpose(low)], axis=1)
        return jnp.concatenate([top, jnp.concatenate([low, gram_ref[at, 2 * half:, :]], axis=1)], axis=0)

    running = unfold(0)
    own[0] = running
    for l in range(depth):
        g = unfold(l + 1)
        sib[l] = g if l == 0 else reorder(g, total[l - 1])
        running = running + g
        own[l + 1] = reorder(running, total[l])

    def dense(s):
        if s <= depth:
            return own, s
        return sib, min(s - depth - 1, depth - 1)

    for j in range(steps):
        for g in range(groups):
            lo = NB * j
            pieces = []
            for t in range(4):
                ref, at = dense(min(4 * g + t, slots - 1))
                pieces.append(ref[at, lo:lo + NB, :])
            panel[g, j] = jnp.concatenate(pieces, axis=0).T

    lane = lax.broadcasted_iota(jnp.int32, (NB, 128), 1)
    rows = lax.broadcasted_iota(jnp.int32, (NB, 128), 0)
    seg_base = (lane // NB) * NB
    r128 = lax.broadcasted_iota(jnp.int32, (128, 128), 0) // NB
    l128 = lax.broadcasted_iota(jnp.int32, (128, 128), 1) // NB
    same = r128 == l128

    def spread(x):
        return jnp.where(same, jnp.concatenate([x] * 4, axis=0), 0.0)

    for j in range(steps):
        lo = NB * j
        nxt = lo + NB
        for g in range(groups):
            d = panel[g, j, lo:nxt, :]
            li = diag_inverse(d, seg_base, rows)
            lp = dotf(panel[g, j, lo:, :], spread(li), NT)
            top = jnp.where(lane - seg_base <= rows, lp[:NB], 0.0)
            if lo:
                panel[g, j, :lo, :] = jnp.zeros((lo, 128), f32)
            panel[g, j, lo:nxt, :] = top
            if nxt < size:
                panel[g, j, nxt:, :] = lp[NB:]
                low = lp[NB:]
                lowh = halves(low)
                for i in range(j + 1, steps):
                    at = NB * (i - j - 1)
                    rhs = halves(spread(low[at:at + NB]))
                    panel[g, i, NB * i:, :] -= dot3((lowh[0][at:], lowh[1][at:]), rhs, NT)
            if g < n_inv_groups:
                lih = halves(li)
                for c in range(j + 1):
                    if c == j:
                        x = li
                    else:
                        x = dot3(lih, halves(spread(inv[g, c, lo:nxt, :])), NN)
                    inv[g, c, lo:nxt, :] = x
                    if nxt < size:
                        upd = dot3(lowh, halves(spread(x)), NN)
                        if c == j:
                            inv[g, c, nxt:, :] = -upd
                        else:
                            inv[g, c, nxt:, :] -= upd
                if lo:
                    inv[g, j, :lo, :] = jnp.zeros((lo, 128), f32)

    for j in range(steps):
        for g in range(groups):
            flat = panel[g, j].T
            for t in range(4):
                if 4 * g + t < slots:
                    fact[4 * g + t, NB * j:NB * j + NB, :] = flat[NB * t:NB * t + NB]
            if g < n_inv_groups:
                flat = inv[g, j].T
                for t in range(4):
                    if 4 * g + t <= depth:
                        finv[4 * g + t, NB * j:NB * j + NB, :] = flat[NB * t:NB * t + NB]

    basis_ref[...] = dotf(finv[0] * math.sqrt(rhs_ref.shape[1] * lax.axis_size("blk")), rhs_ref[...], TN)
    for l in range(depth):
        v = halves(pick(finv[l + 1] * math.sqrt(2 * size), hot[l], NN, False))
        second = second_ref[l]
        trans_ref[l, pl.ds(pl.multiple_of(second * size, size), size), :] = dot3(halves(fact[l]), v, NN)
        trans_ref[l, pl.ds(pl.multiple_of((1 - second) * size, size), size), :] = dot3(
            halves(fact[depth + 1 + l]), v, NN)


def tri(order, grams, second, rhs):
    depth, size = order.shape
    return pl.pallas_call(
        functools.partial(tri_kernel, 2),
        out_shape=(jax.ShapeDtypeStruct(rhs.shape, f32), jax.ShapeDtypeStruct((depth, 2 * size, size), f32)),
        in_specs=[pl.BlockSpec(memory_space=pltpu.VMEM), pl.BlockSpec(memory_space=pltpu.VMEM),
                  pl.BlockSpec(memory_space=pltpu.SMEM), pl.BlockSpec(memory_space=pltpu.VMEM)],
        out_specs=[pl.BlockSpec(memory_space=pltpu.VMEM)] * 2,
        scratch_shapes=[
            pltpu.VMEM((depth + 1, size, size), f32),
            pltpu.VMEM((depth, size, size), f32),
            pltpu.VMEM((4, 8, size, 128), f32),
            pltpu.VMEM((2, 8, size, 128), f32),
            pltpu.VMEM((2 * depth + 1, size, size), f32),
            pltpu.VMEM((depth + 1, size, size), f32),
        ],
        compiler_params=pltpu.CompilerParams(vmem_limit_bytes=48 << 20),
    )(order, grams, second, rhs)


MESH = pl.DeviceIdType.MESH


def sums_kernel(gram_ref, out_ref, flat, part, run, got, stage, full,
                part_send, part_recv, got_send, got_recv, fwd_send, fwd_recv):
    leaf, blk = lax.axis_index("leaf"), lax.axis_index("blk")
    n_blk = lax.axis_size("blk")
    rounds = run.shape[0]
    half = flat.shape[1]
    piece = run.shape[1]

    def mates(r):
        unit = 4 ** r
        digit = (leaf // unit) % 4
        moved = (digit + 1 - 2 * (digit % 2), digit + 2 - 4 * (digit // 2), 3 - digit)
        return [leaf + (m - digit) * unit for m in moved]

    barrier = pltpu.get_barrier_semaphore()
    for d in range(1, n_blk):
        pl.semaphore_signal(barrier, inc=1, device_id=(leaf, (blk + d) % n_blk), device_id_type=MESH)
    for r in range(rounds):
        for mate in mates(r):
            pl.semaphore_signal(barrier, inc=1, device_id=(mate, blk), device_id_type=MESH)
    flat[0:half] = gram_ref[0:half, 0:half]
    flat[half:2 * half] = gram_ref[half:, 0:half]
    flat[2 * half:] = gram_ref[half:, half:]
    pl.semaphore_wait(barrier, n_blk - 1 + 3 * rounds)

    started = []

    def send(src, dst, s_sem, r_sem, device):
        copy = pltpu.make_async_remote_copy(src_ref=src, dst_ref=dst, send_sem=s_sem, recv_sem=r_sem,
                                            device_id=device, device_id_type=MESH)
        copy.start()
        started.append(copy)
        return copy

    first = []
    for d in range(1, n_blk):
        peer = (blk + d) % n_blk
        first.append(send(flat.at[pl.ds(pl.multiple_of(peer * piece, 8), piece)], part.at[d - 1],
                          part_send.at[d - 1], part_recv.at[d - 1], (leaf, peer)))
    for copy in first:
        copy.wait_recv()
    mine = pl.multiple_of(blk * piece, 8)
    run[0] = flat[pl.ds(mine, piece)] + ((part[0] + part[1]) + part[2])
    stage[0] = run[0]
    full[0, pl.ds(mine, piece)] = stage[0]
    forwards = []
    for r in range(rounds):
        copies = [send(run.at[r], got.at[r, m], got_send.at[r, m], got_recv.at[r, m], (mate, blk))
                  for m, mate in enumerate(mates(r))]
        if r == 0:
            for d in range(1, n_blk):
                forwards.append(send(stage.at[0], full.at[0, pl.ds(mine, piece)], fwd_send.at[0, d - 1],
                                     fwd_recv.at[0, d - 1], (leaf, (blk + d) % n_blk)))
        for copy in copies:
            copy.wait_recv()
        near = got[r, 0]
        far = got[r, 1] + got[r, 2]
        if r + 1 < rounds:
            run[r + 1] = run[r] + near + far
        for k, value in enumerate((near, far)):
            at = 1 + 2 * r + k
            stage[at] = value
            full[at, pl.ds(mine, piece)] = value
        for k in range(2):
            at = 1 + 2 * r + k
            for d in range(1, n_blk):
                forwards.append(send(stage.at[at], full.at[at, pl.ds(mine, piece)], fwd_send.at[at, d - 1],
                                     fwd_recv.at[at, d - 1], (leaf, (blk + d) % n_blk)))
    for copy in forwards:
        copy.wait_recv()
    for copy in started:
        copy.wait_send()
    out_ref[...] = full[...]


def subtree_sums(gram, depth):
    size = gram.shape[0]
    half = size // 2
    rows = 3 * half
    n_blk = 4
    piece = rows // n_blk
    rounds = depth // 2
    vm = lambda *shape: pltpu.VMEM(shape, f32)
    return pl.pallas_call(
        sums_kernel,
        out_shape=jax.ShapeDtypeStruct((depth + 1, rows, half), f32),
        in_specs=[pl.BlockSpec(memory_space=pltpu.VMEM)],
        out_specs=pl.BlockSpec(memory_space=pltpu.VMEM),
        scratch_shapes=[
            vm(rows, half), vm(n_blk - 1, piece, half), vm(rounds, piece, half), vm(rounds, 3, piece, half),
            vm(depth + 1, piece, half), vm(depth + 1, rows, half),
            pltpu.SemaphoreType.DMA((n_blk - 1,)), pltpu.SemaphoreType.DMA((n_blk - 1,)),
            pltpu.SemaphoreType.DMA((rounds, 3)), pltpu.SemaphoreType.DMA((rounds, 3)),
            pltpu.SemaphoreType.DMA((depth + 1, n_blk - 1)), pltpu.SemaphoreType.DMA((depth + 1, n_blk - 1)),
        ],
        compiler_params=pltpu.CompilerParams(collective_id=1, has_side_effects=True, vmem_limit_bytes=16 << 20),
    )(gram)


def near_kernel(dims, slot_ref, feat_ref, sketch_ref, omega_ref, gram_ref, rhs_ref,
                hot, out_a, out_b, in_a, in_b, side, acc, row_aug,
                send_a, recv_a, send_b, recv_b, side_send, side_recv):
    count_x, count_z, count_core = dims
    count = count_x * count_z * count_core
    leaf, blk = lax.axis_index("leaf"), lax.axis_index("blk")
    n_blk = lax.axis_size("blk")
    points = slot_ref.shape[1]
    chunk = points // count
    feats = feat_ref.shape[0]
    rank = omega_ref.shape[0]
    tail = out_a.shape[1] - rank
    groups = 4
    per = count // groups
    wide = points // groups
    my_core = leaf % count_core
    my_z = (leaf // count_core) % count_z
    my_x = leaf // (count_core * count_z)
    right, left = (blk + 1) % n_blk, (blk + n_blk - 1) % n_blk

    def target(t):
        dz = (t * 3) % count_z
        a = t // count_z
        dx = (a + t) % count_x
        dc = (a // count_x + t) % count_core
        return (((my_x + dx) % count_x) * count_z + (my_z + dz) % count_z) * count_core + (my_core + dc) % count_core

    barrier = pltpu.get_barrier_semaphore()

    @pl.loop(1, count)
    def _(t):
        pl.semaphore_signal(barrier, inc=1, device_id=(target(t), blk), device_id_type=MESH)

    for peer in (right, left):
        pl.semaphore_signal(barrier, inc=1, device_id=(leaf, peer), device_id_type=MESH)

    own_row = slot_ref[...].astype(f32)
    own_col = jnp.transpose(jnp.broadcast_to(own_row, (128, points)))
    for c in range(points // 128):
        piece = own_row[:, 128 * c:128 * c + 128]
        place = jnp.sum(jnp.where(own_col < piece, 1.0, 0.0), axis=0, keepdims=True).astype(jnp.int32)
        at = lax.broadcasted_iota(jnp.int32, (points, 128), 0)
        hot[:, 128 * c:128 * c + 128] = jnp.where(at == place, 1.0, 0.0).astype(bf16)

    place_row = (slot_ref[...] % points).astype(f32)
    extra = jnp.concatenate(
        [feat_ref[...], place_row, jnp.zeros((tail - feats - 1, points), f32)], axis=0)
    eh, el = halves(extra)
    oh, ol = halves(omega_ref[...])

    def sort_rows(r, hi, lo):
        h = hot[pl.ds(pl.multiple_of(r * 128, 128), 128), :]
        return mm(h, hi, NT) + mm(h, lo, NT)

    for r in range(points // 128):
        out_a[128 * r:128 * r + 128, 0:rank] = sort_rows(r, oh, ol)
        out_a[128 * r:128 * r + 128, rank:] = sort_rows(r, eh, el)

    pl.semaphore_wait(barrier, count - 1 + 2)

    def to_leaf(t, out, into, s_sem, r_sem):
        goal = target(t)
        return pltpu.make_async_remote_copy(
            src_ref=out.at[pl.ds(pl.multiple_of(goal * chunk, chunk), chunk)],
            dst_ref=into.at[pl.ds(pl.multiple_of(t * chunk, chunk), chunk)],
            send_sem=s_sem.at[t], recv_sem=r_sem.at[t], device_id=(goal, blk), device_id_type=MESH)

    @pl.loop(1, count)
    def _(t):
        to_leaf(t, out_a, in_a, send_a, recv_a).start()

    sh, sl = halves(sketch_ref[...])
    for r in range(points // 128):
        out_b[128 * r:128 * r + 128, :] = sort_rows(r, sh, sl)

    @pl.loop(1, count)
    def _(t):
        to_leaf(t, out_b, in_b, send_b, recv_b).start()

    own_rows = pl.ds(pl.multiple_of(leaf * chunk, chunk), chunk)
    in_a[0:chunk] = out_a[own_rows, :]
    in_b[0:chunk] = out_b[own_rows, :]

    def own_side(g, way):
        peer, slot_at = ((right, 0), (left, 1))[way]
        rows = pl.ds(g * wide, wide)
        return pltpu.make_async_remote_copy(
            src_ref=in_a.at[rows], dst_ref=side.at[slot_at, rows], send_sem=side_send.at[way, g],
            recv_sem=side_recv.at[slot_at, g], device_id=(leaf, peer), device_id_type=MESH)

    def relay(g, way):
        peer = (right, left)[way]
        rows = pl.ds(g * wide + way * (wide // 2), wide // 2)
        return pltpu.make_async_remote_copy(
            src_ref=side.at[way, rows], dst_ref=side.at[2, rows], send_sem=side_send.at[2 + way, g],
            recv_sem=side_recv.at[2 + way, g], device_id=(leaf, peer), device_id_type=MESH)

    scale = -2.0 / feats * math.log2(math.e)

    def arrive(g):
        @pl.loop(max(1, g * per), (g + 1) * per)
        def _(t):
            to_leaf(t, out_a, in_a, send_a, recv_a).wait_recv()
        own_side(g, 0).start()
        own_side(g, 1).start()
        x = in_a[g * wide:g * wide + wide, rank:rank + feats]
        xh, xl = halves(x)
        norm = thirds(jnp.sum(x * x, axis=1, keepdims=True) * scale)
        one = jnp.ones((wide, 1), bf16)
        sh_, sl_ = halves(x * (-2.0 * scale))
        row_aug[g * wide:g * wide + wide, :] = jnp.concatenate(
            [sh_, sh_, sl_, *norm, one, one, one, jnp.zeros((wide, 256 - 3 * feats - 6), bf16)], axis=1)

    def hand_on(g):
        own_side(g, 0).wait_recv()
        relay(g, 0).start()
        own_side(g, 1).wait_recv()
        relay(g, 1).start()

    def absorb(block):
        x = block[:, rank:rank + feats]
        xh, xl = halves(x)
        norm = thirds(jnp.sum(x * x, axis=1, keepdims=True) * scale)
        one = jnp.ones((wide, 1), bf16)
        col_aug = jnp.concatenate(
            [xh, xl, xh, one, one, one, *norm, jnp.zeros((wide, 256 - 3 * feats - 6), bf16)], axis=1)
        om = halves(block[:, 0:rank])
        for a in range(groups):
            rows = slice(a * wide, a * wide + wide)
            value = jnp.exp2(mm(row_aug[rows, :], col_aug, NT))
            acc[rows, :] += dot3(halves(value), om, NN)

    arrive(0)
    for g in range(1, groups):
        arrive(g)
        hand_on(g - 1)
    acc[...] = jnp.zeros_like(acc)

    @pl.loop(0, groups)
    def _(g):
        absorb(in_a[pl.ds(pl.multiple_of(g * wide, wide), wide), :])

    hand_on(groups - 1)

    @pl.loop(0, 2 * groups)
    def _(i):
        absorb(side[i // groups, pl.ds(pl.multiple_of((i % groups) * wide, wide), wide), :])

    @pl.loop(0, groups)
    def _(g):
        relay(g, 0).wait_recv()
        relay(g, 1).wait_recv()
        absorb(side[2, pl.ds(pl.multiple_of(g * wide, wide), wide), :])

    @pl.loop(1, count)
    def _(t):
        to_leaf(t, out_b, in_b, send_b, recv_b).wait_recv()

    off = halves(in_b[...] - acc[...])
    gram_ref[...] = dot3(off, off, TN)
    back = jnp.where(
        in_a[:, rank + feats:rank + feats + 1].astype(jnp.int32) == lax.broadcasted_iota(jnp.int32, (points, points), 1),
        1.0, 0.0).astype(bf16)
    rhs_ref[...] = mm(off[0], back, TN) + mm(off[1], back, TN)

    @pl.loop(1, count)
    def _(t):
        to_leaf(t, out_a, in_a, send_a, recv_a).wait_send()
        to_leaf(t, out_b, in_b, send_b, recv_b).wait_send()

    @pl.loop(0, groups)
    def _(g):
        for way in range(2):
            own_side(g, way).wait_send()
            relay(g, way).wait_send()


def near_field(slot, features, sketch, omega):
    feats, points = features.shape
    rank = sketch.shape[0]
    count = lax.axis_size("leaf")
    core = 2
    z = min(8, count // core)
    dims = (count // (core * z), z, core)
    width = rank + 128
    vm = lambda *shape: pltpu.VMEM(shape, f32)
    dma = lambda *shape: pltpu.SemaphoreType.DMA(shape)
    return pl.pallas_call(
        functools.partial(near_kernel, dims),
        out_shape=(jax.ShapeDtypeStruct((rank, rank), f32), jax.ShapeDtypeStruct((rank, points), f32)),
        in_specs=[pl.BlockSpec(memory_space=pltpu.VMEM)] * 4,
        out_specs=[pl.BlockSpec(memory_space=pltpu.VMEM)] * 2,
        scratch_shapes=[
            pltpu.VMEM((points, points), bf16),
            vm(points, width), vm(points, rank), vm(points, width), vm(points, rank),
            vm(3, points, width), vm(points, rank), pltpu.VMEM((points, 256), bf16),
            dma(count), dma(count), dma(count), dma(count), dma(4, 4), dma(4, 4),
        ],
        compiler_params=pltpu.CompilerParams(collective_id=0, has_side_effects=True, vmem_limit_bytes=52 << 20),
    )(slot[None], features, sketch, omega)


def per_device(features, sketch, omega, slot, column_order):
    depth = column_order.shape[0]
    gram, turned = near_field(slot, features, sketch, omega)
    sums = subtree_sums(gram, depth)
    second = lax.axis_index("leaf") >> jnp.arange(depth, dtype=jnp.int32) & 1
    leaf_basis, transfers = tri(column_order, sums, second, turned)
    return (leaf_basis, transfers[None])


def solution(mesh):
    placed = (
        P(None, ("leaf", "blk")),
        P(None, ("leaf", "blk")),
        P(None, ("leaf", "blk")),
        P(("leaf", "blk")),
        P(),
    )
    return jax.shard_map(
        per_device,
        mesh=mesh,
        in_specs=placed,
        out_specs=(P(None, ("leaf", "blk")), P("leaf", None, None, None)),
        check_vma=False,
    )
```

```python
import functools
import math

import jax
import jax.numpy as jnp
from jax import lax
from jax.experimental import pallas as pl
from jax.experimental.pallas import tpu as pltpu
from jax.sharding import PartitionSpec as P

NN = (((1,), (0,)), ((), ()))
NT = (((1,), (1,)), ((), ()))
TN = (((0,), (0,)), ((), ()))
f32, bf16 = jnp.float32, jnp.bfloat16


def mm(a, b, dims):
    return lax.dot_general(a, b, dims, preferred_element_type=f32)


def halves(x):
    hi = x.astype(bf16)
    return hi, (x - hi.astype(f32)).astype(bf16)


def thirds(x):
    hi = x.astype(bf16)
    rest = x - hi.astype(f32)
    mid = rest.astype(bf16)
    return hi, mid, (rest - mid.astype(f32)).astype(bf16)


def dot3(a, b, dims):
    return mm(a[0], b[0], dims) + (mm(a[0], b[1], dims) + mm(a[1], b[0], dims))


def dotf(a, b, dims):
    return dot3(halves(a), halves(b), dims)


def pick(x, hot, dims, left):
    parts = thirds(x)
    if left:
        return mm(parts[0], hot, dims) + mm(parts[1], hot, dims) + mm(parts[2], hot, dims)
    return mm(hot, parts[0], dims) + mm(hot, parts[1], dims) + mm(hot, parts[2], dims)


NB = 32
TILE = 8


def spread_row(x, i):
    return jnp.broadcast_to(x[i:i + 1, :], x.shape)


def diag_inverses(blocks):
    tiles = NB // TILE
    width = 128 * len(blocks)
    a = [jnp.concatenate([x[TILE * q:TILE * q + TILE] for x in blocks], axis=1) for q in range(tiles)]
    lane = lax.broadcasted_iota(jnp.int32, (TILE, width), 1) % NB
    row = lax.broadcasted_iota(jnp.int32, (TILE, width), 0)
    base = lax.broadcasted_iota(jnp.int32, (TILE, 128), 1) // NB * NB
    b = [jnp.where(lane == row + TILE * q, 1.0, 0.0).astype(f32) for q in range(tiles)]

    def column(x, k):
        return jnp.concatenate(
            [jnp.take_along_axis(x[:, 128 * g:128 * g + 128], base + k, axis=1, mode="promise_in_bounds")
             for g in range(len(blocks))], axis=1)

    done = []
    for p in range(tiles):
        below = range(p, tiles)
        cols = [{q: column(a[q], TILE * p + i) for q in below} for i in range(TILE)]
        mult = []
        scale = jnp.zeros((TILE, width), f32)
        for i in range(TILE):
            root = lax.rsqrt(spread_row(cols[i][p], i))
            scale = jnp.where(row == i, root, scale)
            m = {q: cols[i][q] * (root * root) for q in below}
            m[p] = jnp.where(row > i, m[p], 0.0)
            mult.append(m)
            for t in range(i + 1, TILE):
                head = spread_row(cols[t][p], i)
                for q in below:
                    cols[t][q] = cols[t][q] - m[q] * head
            if i + 1 < TILE:
                a[p] = a[p] - m[p] * spread_row(a[p], i)
                b[p] = b[p] - m[p] * spread_row(b[p], i)
        for i in range(TILE):
            ra, rb = spread_row(a[p], i), spread_row(b[p], i)
            for q in range(p + 1, tiles):
                a[q] = a[q] - mult[i][q] * ra
                b[q] = b[q] - mult[i][q] * rb
        done.append(b[p] * scale)
    whole = jnp.concatenate(done, axis=0)
    return [whole[:, 128 * g:128 * g + 128] for g in range(len(blocks))]


def tri_kernel(n_inv_groups, order_ref, gram_ref, second_ref, rhs_ref, basis_ref, trans_ref,
               own, sib, panel, inv, fact, finv):
    groups = 4
    size = order_ref.shape[1]
    half = size // 2
    steps = size // NB
    depth = order_ref.shape[0]
    slots = 2 * depth + 1
    isub = lax.broadcasted_iota(jnp.int32, (size, size), 0)
    hot = [jnp.where(isub == order_ref[l:l + 1, :], 1.0, 0.0).astype(bf16) for l in range(depth)]
    total = [hot[0]]
    for l in range(1, depth):
        total.append(mm(total[-1], hot[l], NN).astype(bf16))

    def reorder(g, q):
        return pick(pick(g, q, NN, True), q, TN, False)

    def unfold(at):
        low = gram_ref[at, half:2 * half, :]
        top = jnp.concatenate([gram_ref[at, 0:half, :], jnp.transpose(low)], axis=1)
        return jnp.concatenate([top, jnp.concatenate([low, gram_ref[at, 2 * half:, :]], axis=1)], axis=0)

    running = unfold(0)
    own[0] = running
    for l in range(depth):
        g = unfold(l + 1)
        sib[l] = g if l == 0 else reorder(g, total[l - 1])
        running = running + g
        own[l + 1] = reorder(running, total[l])

    def dense(s):
        if s <= depth:
            return own, s
        return sib, min(s - depth - 1, depth - 1)

    for j in range(steps):
        for g in range(groups):
            lo = NB * j
            pieces = []
            for t in range(4):
                ref, at = dense(min(4 * g + t, slots - 1))
                pieces.append(ref[at, lo:lo + NB, :])
            panel[g, j] = jnp.concatenate(pieces, axis=0).T

    lane = lax.broadcasted_iota(jnp.int32, (NB, 128), 1)
    rows = lax.broadcasted_iota(jnp.int32, (NB, 128), 0)
    seg_base = (lane // NB) * NB
    r128 = lax.broadcasted_iota(jnp.int32, (128, 128), 0) // NB
    l128 = lax.broadcasted_iota(jnp.int32, (128, 128), 1) // NB
    same = r128 == l128

    def spread(x):
        return jnp.where(same, jnp.concatenate([x] * 4, axis=0), 0.0)

    for j in range(steps):
        lo = NB * j
        nxt = lo + NB
        inverses = diag_inverses([panel[g, j, lo:nxt, :] for g in range(groups)])
        for g in range(groups):
            li = inverses[g]
            lp = dotf(panel[g, j, lo:, :], spread(li), NT)
            top = jnp.where(lane - seg_base <= rows, lp[:NB], 0.0)
            if lo:
                panel[g, j, :lo, :] = jnp.zeros((lo, 128), f32)
            panel[g, j, lo:nxt, :] = top
            if nxt < size:
                panel[g, j, nxt:, :] = lp[NB:]
                low = lp[NB:]
                lowh = halves(low)
                for i in range(j + 1, steps):
                    at = NB * (i - j - 1)
                    rhs = halves(spread(low[at:at + NB]))
                    panel[g, i, NB * i:, :] -= dot3((lowh[0][at:], lowh[1][at:]), rhs, NT)
            if g < n_inv_groups:
                lih = halves(li)
                for c in range(j + 1):
                    if c == j:
                        x = li
                    else:
                        x = dot3(lih, halves(spread(inv[g, c, lo:nxt, :])), NN)
                    inv[g, c, lo:nxt, :] = x
                    if nxt < size:
                        upd = dot3(lowh, halves(spread(x)), NN)
                        if c == j:
                            inv[g, c, nxt:, :] = -upd
                        else:
                            inv[g, c, nxt:, :] -= upd
                if lo:
                    inv[g, j, :lo, :] = jnp.zeros((lo, 128), f32)

    for j in range(steps):
        for g in range(groups):
            flat = panel[g, j].T
            for t in range(4):
                if 4 * g + t < slots:
                    fact[4 * g + t, NB * j:NB * j + NB, :] = flat[NB * t:NB * t + NB]
            if g < n_inv_groups:
                flat = inv[g, j].T
                for t in range(4):
                    if 4 * g + t <= depth:
                        finv[4 * g + t, NB * j:NB * j + NB, :] = flat[NB * t:NB * t + NB]

    whole = jnp.transpose(finv[0]) * math.sqrt(rhs_ref.shape[0] * lax.axis_size("blk"))
    basis_ref[...] = dotf(whole, rhs_ref[...], NT)
    for l in range(depth):
        v = halves(pick(finv[l + 1] * math.sqrt(2 * size), hot[l], NN, False))
        second = second_ref[l]
        trans_ref[l, pl.ds(pl.multiple_of(second * size, size), size), :] = dot3(halves(fact[l]), v, NN)
        trans_ref[l, pl.ds(pl.multiple_of((1 - second) * size, size), size), :] = dot3(
            halves(fact[depth + 1 + l]), v, NN)


def tri(order, grams, second, rhs):
    depth, size = order.shape
    return pl.pallas_call(
        functools.partial(tri_kernel, 2),
        out_shape=(jax.ShapeDtypeStruct(rhs.shape[::-1], f32), jax.ShapeDtypeStruct((depth, 2 * size, size), f32)),
        in_specs=[pl.BlockSpec(memory_space=pltpu.VMEM), pl.BlockSpec(memory_space=pltpu.VMEM),
                  pl.BlockSpec(memory_space=pltpu.SMEM), pl.BlockSpec(memory_space=pltpu.VMEM)],
        out_specs=[pl.BlockSpec(memory_space=pltpu.VMEM)] * 2,
        scratch_shapes=[
            pltpu.VMEM((depth + 1, size, size), f32),
            pltpu.VMEM((depth, size, size), f32),
            pltpu.VMEM((4, 8, size, 128), f32),
            pltpu.VMEM((2, 8, size, 128), f32),
            pltpu.VMEM((2 * depth + 1, size, size), f32),
            pltpu.VMEM((depth + 1, size, size), f32),
        ],
        compiler_params=pltpu.CompilerParams(vmem_limit_bytes=48 << 20),
    )(order, grams, second, rhs)


MESH = pl.DeviceIdType.MESH


def sums_kernel(gram_ref, out_ref, flat, part, run, got, stage, full,
                part_send, part_recv, got_send, got_recv, fwd_send, fwd_recv):
    leaf, blk = lax.axis_index("leaf"), lax.axis_index("blk")
    n_blk = lax.axis_size("blk")
    rounds = run.shape[0]
    half = flat.shape[1]
    piece = run.shape[1]

    def mates(r):
        unit = 4 ** r
        digit = (leaf // unit) % 4
        moved = (digit + 1 - 2 * (digit % 2), digit + 2 - 4 * (digit // 2), 3 - digit)
        return [leaf + (m - digit) * unit for m in moved]

    barrier = pltpu.get_barrier_semaphore()
    for d in range(1, n_blk):
        pl.semaphore_signal(barrier, inc=1, device_id=(leaf, (blk + d) % n_blk), device_id_type=MESH)
    for r in range(rounds):
        for mate in mates(r):
            pl.semaphore_signal(barrier, inc=1, device_id=(mate, blk), device_id_type=MESH)
    flat[0:half] = gram_ref[0:half, 0:half]
    flat[half:2 * half] = gram_ref[half:, 0:half]
    flat[2 * half:] = gram_ref[half:, half:]
    pl.semaphore_wait(barrier, n_blk - 1 + 3 * rounds)

    started = []

    def send(src, dst, s_sem, r_sem, device):
        copy = pltpu.make_async_remote_copy(src_ref=src, dst_ref=dst, send_sem=s_sem, recv_sem=r_sem,
                                            device_id=device, device_id_type=MESH)
        copy.start()
        started.append(copy)
        return copy

    first = []
    for d in range(1, n_blk):
        peer = (blk + d) % n_blk
        first.append(send(flat.at[pl.ds(pl.multiple_of(peer * piece, 8), piece)], part.at[d - 1],
                          part_send.at[d - 1], part_recv.at[d - 1], (leaf, peer)))
    for copy in first:
        copy.wait_recv()
    mine = pl.multiple_of(blk * piece, 8)
    run[0] = flat[pl.ds(mine, piece)] + ((part[0] + part[1]) + part[2])
    stage[0] = run[0]
    full[0, pl.ds(mine, piece)] = stage[0]
    forwards = []
    for r in range(rounds):
        copies = [send(run.at[r], got.at[r, m], got_send.at[r, m], got_recv.at[r, m], (mate, blk))
                  for m, mate in enumerate(mates(r))]
        if r == 0:
            for d in range(1, n_blk):
                forwards.append(send(stage.at[0], full.at[0, pl.ds(mine, piece)], fwd_send.at[0, d - 1],
                                     fwd_recv.at[0, d - 1], (leaf, (blk + d) % n_blk)))
        for copy in copies:
            copy.wait_recv()
        near = got[r, 0]
        far = got[r, 1] + got[r, 2]
        if r + 1 < rounds:
            run[r + 1] = run[r] + near + far
        for k, value in enumerate((near, far)):
            at = 1 + 2 * r + k
            stage[at] = value
            full[at, pl.ds(mine, piece)] = value
        for k in range(2):
            at = 1 + 2 * r + k
            for d in range(1, n_blk):
                forwards.append(send(stage.at[at], full.at[at, pl.ds(mine, piece)], fwd_send.at[at, d - 1],
                                     fwd_recv.at[at, d - 1], (leaf, (blk + d) % n_blk)))
    for copy in forwards:
        copy.wait_recv()
    for copy in started:
        copy.wait_send()
    out_ref[...] = full[...]


def subtree_sums(gram, depth):
    size = gram.shape[0]
    half = size // 2
    rows = 3 * half
    n_blk = 4
    piece = rows // n_blk
    rounds = depth // 2
    vm = lambda *shape: pltpu.VMEM(shape, f32)
    return pl.pallas_call(
        sums_kernel,
        out_shape=jax.ShapeDtypeStruct((depth + 1, rows, half), f32),
        in_specs=[pl.BlockSpec(memory_space=pltpu.VMEM)],
        out_specs=pl.BlockSpec(memory_space=pltpu.VMEM),
        scratch_shapes=[
            vm(rows, half), vm(n_blk - 1, piece, half), vm(rounds, piece, half), vm(rounds, 3, piece, half),
            vm(depth + 1, piece, half), vm(depth + 1, rows, half),
            pltpu.SemaphoreType.DMA((n_blk - 1,)), pltpu.SemaphoreType.DMA((n_blk - 1,)),
            pltpu.SemaphoreType.DMA((rounds, 3)), pltpu.SemaphoreType.DMA((rounds, 3)),
            pltpu.SemaphoreType.DMA((depth + 1, n_blk - 1)), pltpu.SemaphoreType.DMA((depth + 1, n_blk - 1)),
        ],
        compiler_params=pltpu.CompilerParams(collective_id=1, has_side_effects=True, vmem_limit_bytes=16 << 20),
    )(gram)


def near_kernel(dims, slot_ref, feat_ref, sketch_ref, omega_ref, gram_ref, rhs_ref,
                hot, back, out_o, out_f, out_p, out_s, in_o, in_f, in_p, in_s, side_o, side_f, acc, row_aug,
                send_sem, recv_sem, side_send, side_recv):
    count_x, count_z, count_core = dims
    count = count_x * count_z * count_core
    leaf, blk = lax.axis_index("leaf"), lax.axis_index("blk")
    n_blk = lax.axis_size("blk")
    points = slot_ref.shape[1]
    chunk = points // count
    feats = feat_ref.shape[0]
    groups = 4
    per = count // groups
    wide = points // groups
    strip = min(128, wide)
    in_strip = strip // chunk
    my_core = leaf % count_core
    my_z = (leaf // count_core) % count_z
    my_x = leaf // (count_core * count_z)
    right, left = (blk + 1) % n_blk, (blk + n_blk - 1) % n_blk

    def target(t):
        dz = (t * 3) % count_z
        a = t // count_z
        dx = (a + t) % count_x
        dc = (a // count_x + t) % count_core
        return (((my_x + dx) % count_x) * count_z + (my_z + dz) % count_z) * count_core + (my_core + dc) % count_core

    barrier = pltpu.get_barrier_semaphore()

    @pl.loop(1, count)
    def _(t):
        pl.semaphore_signal(barrier, inc=1, device_id=(target(t), blk), device_id_type=MESH)

    for peer in (right, left):
        pl.semaphore_signal(barrier, inc=1, device_id=(leaf, peer), device_id_type=MESH)

    own = slot_ref[...]
    bits = lambda n: n.bit_length() - 1
    goal = own >> bits(points * n_blk)
    dc = ((goal & (count_core - 1)) - my_core) & (count_core - 1)
    dz = (((goal >> bits(count_core)) & (count_z - 1)) - my_z) & (count_z - 1)
    dx = ((goal >> bits(count_core * count_z)) - my_x) & (count_x - 1)
    turn = (dz * 3) & (count_z - 1)
    a = ((dx - turn) & (count_x - 1)) + count_x * ((dc - turn) & (count_core - 1))
    shift = chunk * (turn + count_z * a - goal)
    own_row = own.astype(f32)
    own_col = jnp.transpose(jnp.broadcast_to(own_row, (128, points)))
    at = lax.broadcasted_iota(jnp.int32, (points, 128), 0)
    for c in range(points // 128):
        lanes = slice(128 * c, 128 * c + 128)
        place = jnp.sum(jnp.where(own_col < own_row[:, lanes], 1.0, 0.0), axis=0, keepdims=True).astype(jnp.int32)
        hot[:, lanes] = jnp.where(at == place + shift[:, lanes], 1.0, 0.0).astype(bf16)

    fh, fl = halves(jnp.concatenate([feat_ref[...]] * 2, axis=0))
    oh, ol = halves(omega_ref[...])
    pos = jnp.broadcast_to((own & (points - 1)).astype(f32), (16, points))
    ph, plow = halves(pos)
    first = lax.broadcasted_iota(jnp.int32, (8, 2 * feats), 1) < feats

    def moves(t, which):
        src, dst = ((out_o, in_o), (out_f, in_f), (out_p, in_p), (out_s, in_s))[which]
        rows = (chunk, chunk // 2, 1, chunk)[which]
        begin = pl.multiple_of(t * rows, rows)
        source = t // in_strip if which == 2 else begin
        return pltpu.make_async_remote_copy(
            src_ref=src.at[pl.ds(source, rows)], dst_ref=dst.at[pl.ds(begin, rows)],
            send_sem=send_sem.at[which, t], recv_sem=recv_sem.at[which, t],
            device_id=(target(t), blk), device_id_type=MESH)

    for r in range(points // strip):
        rows = slice(strip * r, strip * r + strip)
        h = hot[rows, :]
        out_o[rows, :] = mm(h, oh, NT) + mm(h, ol, NT)
        f = mm(h, fh, NT) + mm(h, fl, NT)
        for c in range(strip // 16):
            out_f[strip // 2 * r + 8 * c:strip // 2 * r + 8 * c + 8, :] = jnp.where(
                first, f[16 * c:16 * c + 8], f[16 * c + 8:16 * c + 16])
        out_p[r] = (mm(ph, h, NT) + mm(plow, h, NT))[0:1]
        if r == 0:
            pl.semaphore_wait(barrier, count - 1 + 2)

        @pl.loop(max(1, in_strip * r), in_strip * r + in_strip)
        def _(t):
            for which in range(3):
                moves(t, which).start()

    sh, sl = halves(sketch_ref[...])
    for r in range(points // strip):
        rows = slice(strip * r, strip * r + strip)
        h = hot[rows, :]
        out_s[rows, :] = mm(h, sh, NT) + mm(h, sl, NT)

        @pl.loop(max(1, in_strip * r), in_strip * r + in_strip)
        def _(t):
            moves(t, 3).start()

    in_o[0:chunk] = out_o[0:chunk]
    in_f[0:chunk // 2] = out_f[0:chunk // 2]
    in_p[0:1] = out_p[0:1]
    in_s[0:chunk] = out_s[0:chunk]

    def own_side(g, way, which):
        peer, slot_at = ((right, 0), (left, 1))[way]
        src, dst, tall = ((in_o, side_o, wide), (in_f, side_f, wide // 2))[which]
        rows = pl.ds(pl.multiple_of(g * tall, tall), tall)
        return pltpu.make_async_remote_copy(
            src_ref=src.at[rows], dst_ref=dst.at[slot_at, rows], send_sem=side_send.at[way, which, g],
            recv_sem=side_recv.at[slot_at, which, g], device_id=(leaf, peer), device_id_type=MESH)

    def relay(g, way, which):
        peer = (right, left)[way]
        ref, tall = ((side_o, wide // 2), (side_f, wide // 4))[which]
        rows = pl.ds(pl.multiple_of((2 * g + way) * tall, tall), tall)
        return pltpu.make_async_remote_copy(
            src_ref=ref.at[way, rows], dst_ref=ref.at[2, rows], send_sem=side_send.at[2 + way, which, g],
            recv_sem=side_recv.at[2 + way, which, g], device_id=(leaf, peer), device_id_type=MESH)

    scale = -2.0 / feats * math.log2(math.e)

    def flat_feats(packed):
        cut = jnp.reshape(packed, (wide // 16, 8, 2 * feats))
        return jnp.reshape(jnp.concatenate([cut[:, :, :feats], cut[:, :, feats:]], axis=1), (wide, feats))

    one = jnp.ones((wide, 1), bf16)
    fill = jnp.zeros((wide, 256 - 3 * feats - 6), bf16)

    def arrive(g):
        @pl.loop(max(1, g * per), (g + 1) * per)
        def _(t):
            for which in range(3):
                moves(t, which).wait_recv()
        for which in range(2):
            for way in range(2):
                own_side(g, way, which).start()
        x = flat_feats(in_f[g * wide // 2:g * wide // 2 + wide // 2, :])
        norm = thirds(jnp.sum(x * x, axis=1, keepdims=True) * scale)
        xh, xl = halves(x * (-2.0 * scale))
        row_aug[g * wide:g * wide + wide, :] = jnp.concatenate([xh, xh, xl, *norm, one, one, one, fill], axis=1)

    def hand_on(g):
        for way in range(2):
            for which in range(2):
                own_side(g, way, which).wait_recv()
                relay(g, way, which).start()

    def absorb(omegas, packed):
        x = flat_feats(packed)
        xh, xl = halves(x)
        norm = thirds(jnp.sum(x * x, axis=1, keepdims=True) * scale)
        col_aug = jnp.concatenate([xh, xl, xh, one, one, one, *norm, fill], axis=1)
        om = halves(omegas)
        for a in range(groups):
            rows = slice(a * wide, a * wide + wide)
            value = jnp.exp2(mm(row_aug[rows, :], col_aug, NT))
            acc[rows, :] += dot3(halves(value), om, NN)

    def rows_of(g, tall):
        return pl.ds(pl.multiple_of(g * tall, tall), tall)

    arrive(0)
    for g in range(1, groups):
        arrive(g)
        hand_on(g - 1)
    acc[...] = jnp.zeros_like(acc)

    @pl.loop(0, groups)
    def _(g):
        absorb(in_o[rows_of(g, wide), :], in_f[rows_of(g, wide // 2), :])

    hand_on(groups - 1)

    sub = lax.broadcasted_iota(jnp.int32, (in_strip, 1, strip), 0)
    lane = lax.broadcasted_iota(jnp.int32, (in_strip, 1, strip), 2)
    down = lax.broadcasted_iota(jnp.int32, (points, strip), 0)
    for u in range(points // strip):
        mine = jnp.where(lane // chunk == sub, in_p[u * in_strip:(u + 1) * in_strip], 0.0)
        row = jnp.sum(mine, axis=0).astype(jnp.int32)
        back[:, u * strip:(u + 1) * strip] = jnp.where(down == row, 1.0, 0.0).astype(bf16)

    @pl.loop(0, 2 * groups)
    def _(i):
        absorb(side_o[i // groups, rows_of(i % groups, wide), :], side_f[i // groups, rows_of(i % groups, wide // 2), :])

    @pl.loop(0, groups)
    def _(g):
        for way in range(2):
            for which in range(2):
                relay(g, way, which).wait_recv()
        absorb(side_o[2, rows_of(g, wide), :], side_f[2, rows_of(g, wide // 2), :])

    for g in range(groups):
        @pl.loop(max(1, g * per), (g + 1) * per)
        def _(t):
            moves(t, 3).wait_recv()
        rows = slice(g * wide, g * wide + wide)
        off = halves(in_s[rows, :] - acc[rows, :])
        term = dot3(off, off, TN)
        spots = back[:, rows]
        moved = mm(spots, off[0], NN) + mm(spots, off[1], NN)
        if g == 0:
            gram_ref[...] = term
            rhs_ref[...] = moved
        else:
            gram_ref[...] += term
            rhs_ref[...] += moved

    @pl.loop(1, count)
    def _(t):
        for which in range(4):
            moves(t, which).wait_send()

    @pl.loop(0, groups)
    def _(g):
        for way in range(2):
            for which in range(2):
                own_side(g, way, which).wait_send()
                relay(g, way, which).wait_send()


def near_field(slot, features, sketch, omega):
    feats, points = features.shape
    rank = sketch.shape[0]
    count = lax.axis_size("leaf")
    core = 2
    z = min(8, count // core)
    dims = (count // (core * z), z, core)
    strip = min(128, points // 4)
    vm = lambda *shape: pltpu.VMEM(shape, f32)
    dma = lambda *shape: pltpu.SemaphoreType.DMA(shape)
    return pl.pallas_call(
        functools.partial(near_kernel, dims),
        out_shape=(jax.ShapeDtypeStruct((rank, rank), f32), jax.ShapeDtypeStruct((points, rank), f32)),
        in_specs=[pl.BlockSpec(memory_space=pltpu.VMEM)] * 4,
        out_specs=[pl.BlockSpec(memory_space=pltpu.VMEM)] * 2,
        scratch_shapes=[
            pltpu.VMEM((points, points), bf16), pltpu.VMEM((points, points), bf16),
            vm(points, rank), vm(points // 2, 2 * feats), vm(points // strip, 1, strip), vm(points, rank),
            vm(points, rank), vm(points // 2, 2 * feats), vm(count, 1, strip), vm(points, rank),
            vm(3, points, rank), vm(3, points // 2, 2 * feats), vm(points, rank), pltpu.VMEM((points, 256), bf16),
            dma(4, count), dma(4, count), dma(4, 2, 4), dma(4, 2, 4),
        ],
        compiler_params=pltpu.CompilerParams(collective_id=0, has_side_effects=True, vmem_limit_bytes=52 << 20),
    )(slot[None], features, sketch, omega)


def per_device(features, sketch, omega, slot, column_order):
    depth = column_order.shape[0]
    gram, turned = near_field(slot, features, sketch, omega)
    sums = subtree_sums(gram, depth)
    second = lax.axis_index("leaf") >> jnp.arange(depth, dtype=jnp.int32) & 1
    leaf_basis, transfers = tri(column_order, sums, second, turned)
    return (leaf_basis, transfers[None])


def solution(mesh):
    placed = (
        P(None, ("leaf", "blk")),
        P(None, ("leaf", "blk")),
        P(None, ("leaf", "blk")),
        P(("leaf", "blk")),
        P(),
    )
    return jax.shard_map(
        per_device,
        mesh=mesh,
        in_specs=placed,
        out_specs=(P(None, ("leaf", "blk")), P("leaf", None, None, None)),
        check_vma=False,
    )
```

```python
import functools
import math

import jax
import jax.numpy as jnp
from jax import lax
from jax.experimental import pallas as pl
from jax.experimental.pallas import tpu as pltpu
from jax.sharding import PartitionSpec as P

NN = (((1,), (0,)), ((), ()))
NT = (((1,), (1,)), ((), ()))
TN = (((0,), (0,)), ((), ()))
f32, bf16 = jnp.float32, jnp.bfloat16


def mm(a, b, dims):
    return lax.dot_general(a, b, dims, preferred_element_type=f32)


def halves(x):
    hi = x.astype(bf16)
    return hi, (x - hi.astype(f32)).astype(bf16)


def thirds(x):
    hi = x.astype(bf16)
    rest = x - hi.astype(f32)
    mid = rest.astype(bf16)
    return hi, mid, (rest - mid.astype(f32)).astype(bf16)


def dot3(a, b, dims):
    return mm(a[0], b[0], dims) + (mm(a[0], b[1], dims) + mm(a[1], b[0], dims))


def dotf(a, b, dims):
    return dot3(halves(a), halves(b), dims)


def pick(x, hot, dims, left):
    hi, lo = halves(x)
    if left:
        return mm(hi, hot, dims) + mm(lo, hot, dims)
    return mm(hot, hi, dims) + mm(hot, lo, dims)


NB = 32
TILE = 8


def spread_row(x, i):
    return jnp.broadcast_to(x[i:i + 1, :], x.shape)


def diag_inverses(blocks):
    tiles = NB // TILE
    width = 128 * len(blocks)
    a = [jnp.concatenate([x[TILE * q:TILE * q + TILE] for x in blocks], axis=1) for q in range(tiles)]
    lane = lax.broadcasted_iota(jnp.int32, (TILE, width), 1) % NB
    row = lax.broadcasted_iota(jnp.int32, (TILE, width), 0)
    base = lax.broadcasted_iota(jnp.int32, (TILE, 128), 1) // NB * NB
    b = [jnp.where(lane == row + TILE * q, 1.0, 0.0).astype(f32) for q in range(tiles)]

    def column(x, k):
        return jnp.concatenate(
            [jnp.take_along_axis(x[:, 128 * g:128 * g + 128], base + k, axis=1, mode="promise_in_bounds")
             for g in range(len(blocks))], axis=1)

    done = []
    for p in range(tiles):
        below = range(p, tiles)
        cols = [{q: column(a[q], TILE * p + i) for q in below} for i in range(TILE)]
        mult = []
        scale = jnp.zeros((TILE, width), f32)
        for i in range(TILE):
            root = lax.rsqrt(spread_row(cols[i][p], i))
            scale = jnp.where(row == i, root, scale)
            m = {q: cols[i][q] * (root * root) for q in below}
            m[p] = jnp.where(row > i, m[p], 0.0)
            mult.append(m)
            for t in range(i + 1, TILE):
                head = spread_row(cols[t][p], i)
                for q in below:
                    cols[t][q] = cols[t][q] - m[q] * head
            if i + 1 < TILE:
                a[p] = a[p] - m[p] * spread_row(a[p], i)
                b[p] = b[p] - m[p] * spread_row(b[p], i)
        for i in range(TILE):
            ra, rb = spread_row(a[p], i), spread_row(b[p], i)
            for q in range(p + 1, tiles):
                a[q] = a[q] - mult[i][q] * ra
                b[q] = b[q] - mult[i][q] * rb
        done.append(b[p] * scale)
    whole = jnp.concatenate(done, axis=0)
    return [whole[:, 128 * g:128 * g + 128] for g in range(len(blocks))]


def tri_kernel(n_inv_groups, order_ref, gram_ref, second_ref, rhs_ref, basis_ref, trans_ref,
               own, sib, panel, inv, fact, finv):
    groups = 4
    size = order_ref.shape[1]
    half = size // 2
    steps = size // NB
    depth = order_ref.shape[0]
    slots = 2 * depth + 1
    isub = lax.broadcasted_iota(jnp.int32, (size, size), 0)
    hot = [jnp.where(isub == order_ref[l:l + 1, :], 1.0, 0.0).astype(bf16) for l in range(depth)]
    total = [hot[0]]
    for l in range(1, depth):
        total.append(mm(total[-1], hot[l], NN).astype(bf16))

    def reorder(g, q):
        return pick(pick(g, q, NN, True), q, TN, False)

    def unfold(at):
        low = gram_ref[at, half:2 * half, :]
        top = jnp.concatenate([gram_ref[at, 0:half, :], jnp.transpose(low)], axis=1)
        return jnp.concatenate([top, jnp.concatenate([low, gram_ref[at, 2 * half:, :]], axis=1)], axis=0)

    running = unfold(0)
    own[0] = running
    for l in range(depth):
        g = unfold(l + 1)
        sib[l] = g if l == 0 else reorder(g, total[l - 1])
        running = running + g
        own[l + 1] = reorder(running, total[l])

    def dense(s):
        if s <= depth:
            return own, s
        return sib, min(s - depth - 1, depth - 1)

    for j in range(steps):
        for g in range(groups):
            lo = NB * j
            pieces = []
            for t in range(4):
                ref, at = dense(min(4 * g + t, slots - 1))
                pieces.append(ref[at, lo:lo + NB, :])
            panel[g, j] = jnp.concatenate(pieces, axis=0).T

    lane = lax.broadcasted_iota(jnp.int32, (NB, 128), 1)
    rows = lax.broadcasted_iota(jnp.int32, (NB, 128), 0)
    seg_base = (lane // NB) * NB
    r128 = lax.broadcasted_iota(jnp.int32, (128, 128), 0) // NB
    l128 = lax.broadcasted_iota(jnp.int32, (128, 128), 1) // NB
    same = r128 == l128

    same = jnp.where(same, 1.0, 0.0).astype(bf16)

    def spread(x):
        return [jnp.concatenate([part] * 4, axis=0) * same for part in halves(x)]

    def spread_all(blocks, axis):
        return [jnp.concatenate(parts, axis=axis) for parts in zip(*[spread(x) for x in blocks])]

    for j in range(steps):
        lo = NB * j
        nxt = lo + NB
        inverses = diag_inverses([panel[g, j, lo:nxt, :] for g in range(groups)])
        for g in range(groups):
            li = inverses[g]
            lp = dot3(halves(panel[g, j, lo:, :]), spread(li), NT)
            top = jnp.where(lane - seg_base <= rows, lp[:NB], 0.0)
            if lo:
                panel[g, j, :lo, :] = jnp.zeros((lo, 128), f32)
            panel[g, j, lo:nxt, :] = top
            if nxt < size:
                panel[g, j, nxt:, :] = lp[NB:]
                low = lp[NB:]
                lowh = halves(low)
                for i in range(j + 1, steps, 2):
                    at = NB * (i - j - 1)
                    pair = range(i, min(i + 2, steps))
                    rhs = spread_all([low[NB * (k - j - 1):NB * (k - j)] for k in pair], 0)
                    upd = dot3((lowh[0][at:], lowh[1][at:]), rhs, NT)
                    for n, k in enumerate(pair):
                        panel[g, k, NB * k:, :] -= upd[NB * n:, 128 * n:128 * n + 128]
            if g < n_inv_groups:
                lih = halves(li)
                for c in range(0, j + 1, 2):
                    pair = [k for k in (c, c + 1) if k < j]
                    xs = []
                    if pair:
                        prod = dot3(lih, spread_all([inv[g, k, lo:nxt, :] for k in pair], 1), NN)
                        xs = [prod[:, 128 * n:128 * n + 128] for n in range(len(pair))]
                    if c + len(pair) == j and len(pair) < 2:
                        pair.append(j)
                        xs.append(li)
                    for k, x in zip(pair, xs):
                        inv[g, k, lo:nxt, :] = x
                    if nxt < size:
                        upd = dot3(lowh, spread_all(xs, 1), NN)
                        for n, k in enumerate(pair):
                            piece = upd[:, 128 * n:128 * n + 128]
                            if k == j:
                                inv[g, k, nxt:, :] = -piece
                            else:
                                inv[g, k, nxt:, :] -= piece
                if lo:
                    inv[g, j, :lo, :] = jnp.zeros((lo, 128), f32)

    for j in range(steps):
        for g in range(groups):
            flat = panel[g, j].T
            for t in range(4):
                if 4 * g + t < slots:
                    fact[4 * g + t, NB * j:NB * j + NB, :] = flat[NB * t:NB * t + NB]
            if g < n_inv_groups:
                flat = inv[g, j].T
                for t in range(4):
                    if 4 * g + t <= depth:
                        finv[4 * g + t, NB * j:NB * j + NB, :] = flat[NB * t:NB * t + NB]

    whole = jnp.transpose(finv[0]) * math.sqrt(rhs_ref.shape[0] * lax.axis_size("blk"))
    basis_ref[...] = dotf(whole, rhs_ref[...], NT)
    for l in range(depth):
        v = halves(pick(finv[l + 1] * math.sqrt(2 * size), hot[l], NN, False))
        second = second_ref[l]
        trans_ref[l, pl.ds(pl.multiple_of(second * size, size), size), :] = dot3(halves(fact[l]), v, NN)
        trans_ref[l, pl.ds(pl.multiple_of((1 - second) * size, size), size), :] = dot3(
            halves(fact[depth + 1 + l]), v, NN)


def tri(order, grams, second, rhs):
    depth, size = order.shape
    return pl.pallas_call(
        functools.partial(tri_kernel, 2),
        out_shape=(jax.ShapeDtypeStruct(rhs.shape[::-1], f32), jax.ShapeDtypeStruct((depth, 2 * size, size), f32)),
        in_specs=[pl.BlockSpec(memory_space=pltpu.VMEM), pl.BlockSpec(memory_space=pltpu.VMEM),
                  pl.BlockSpec(memory_space=pltpu.SMEM), pl.BlockSpec(memory_space=pltpu.VMEM)],
        out_specs=[pl.BlockSpec(memory_space=pltpu.VMEM)] * 2,
        scratch_shapes=[
            pltpu.VMEM((depth + 1, size, size), f32),
            pltpu.VMEM((depth, size, size), f32),
            pltpu.VMEM((4, 8, size, 128), f32),
            pltpu.VMEM((2, 8, size, 128), f32),
            pltpu.VMEM((2 * depth + 1, size, size), f32),
            pltpu.VMEM((depth + 1, size, size), f32),
        ],
        compiler_params=pltpu.CompilerParams(vmem_limit_bytes=48 << 20),
    )(order, grams, second, rhs)


MESH = pl.DeviceIdType.MESH


def sum_subtrees(gram, leaf, blk, out_ref, flat, part, run, got, stage, full, sems):
    part_send, part_recv, got_send, got_recv, fwd_send, fwd_recv = sems
    n_blk = lax.axis_size("blk")
    rounds = run.shape[0]
    half = flat.shape[1]
    piece = run.shape[1]

    def mates(r):
        unit = 4 ** r
        digit = (leaf // unit) % 4
        moved = (digit + 1 - 2 * (digit % 2), digit + 2 - 4 * (digit // 2), 3 - digit)
        return [leaf + (m - digit) * unit for m in moved]

    flat[0:half] = gram[0:half, 0:half]
    flat[half:2 * half] = gram[half:, 0:half]
    flat[2 * half:] = gram[half:, half:]
    started = []

    def send(src, dst, s_sem, r_sem, device):
        copy = pltpu.make_async_remote_copy(src_ref=src, dst_ref=dst, send_sem=s_sem, recv_sem=r_sem,
                                            device_id=device, device_id_type=MESH)
        copy.start()
        started.append(copy)
        return copy

    first = []
    for d in range(1, n_blk):
        peer = (blk + d) % n_blk
        first.append(send(flat.at[pl.ds(pl.multiple_of(peer * piece, 8), piece)], part.at[d - 1],
                          part_send.at[d - 1], part_recv.at[d - 1], (leaf, peer)))
    yield
    mine = pl.multiple_of(blk * piece, 8)
    forwards = []

    def forward(slot_at, begin, size):
        for d in range(1, n_blk):
            forwards.append(send(stage.at[pl.ds(begin, size)], full.at[pl.ds(begin, size), pl.ds(mine, piece)],
                                 fwd_send.at[slot_at, d - 1], fwd_recv.at[slot_at, d - 1], (leaf, (blk + d) % n_blk)))

    for copy in first:
        copy.wait_recv()
    run[0] = flat[pl.ds(mine, piece)] + ((part[0] + part[1]) + part[2])
    for r in range(rounds):
        copies = [send(run.at[r], got.at[r, m], got_send.at[r, m], got_recv.at[r, m], (mate, blk))
                  for m, mate in enumerate(mates(r))]
        if r == 0:
            stage[0] = run[0]
            full[0, pl.ds(mine, piece)] = stage[0]
            forward(0, 0, 1)
        else:
            forward(r, 2 * r - 1, 2)
        for copy in copies:
            copy.wait_recv()
        near = got[r, 0]
        far = got[r, 1] + got[r, 2]
        if r + 1 < rounds:
            run[r + 1] = run[r] + near + far
        for k, value in enumerate((near, far)):
            stage[1 + 2 * r + k] = value
            full[1 + 2 * r + k, pl.ds(mine, piece)] = value
    forward(rounds, 2 * rounds - 1, 2)
    for copy in forwards:
        copy.wait_recv()
    for copy in started:
        copy.wait_send()
    out_ref[...] = full[...]


def near_kernel(dims, slot_ref, feat_ref, sketch_ref, omega_ref, sums_ref, rhs_ref,
                hot, back, out_a, out_p, out_s, in_a, in_p, in_s, side, acc, row_aug, gram, off_hi, off_lo,
                flat, part, run, got, stage, full,
                send_sem, recv_sem, side_send, side_recv, *sum_sems):
    count_x, count_z, count_core = dims
    count = count_x * count_z * count_core
    leaf, blk = lax.axis_index("leaf"), lax.axis_index("blk")
    n_blk = lax.axis_size("blk")
    points = slot_ref.shape[1]
    chunk = points // count
    feats = feat_ref.shape[0]
    groups = 4
    per = count // groups
    rank = omega_ref.shape[0]
    lot = out_a.shape[1]
    low = lot - chunk // 2
    wide = points // groups
    strip = min(128, wide)
    in_strip = strip // chunk
    my_core = leaf % count_core
    my_z = (leaf // count_core) % count_z
    my_x = leaf // (count_core * count_z)
    right, left = (blk + 1) % n_blk, (blk + n_blk - 1) % n_blk

    def target(t):
        a = lax.div(t, count_z)
        core = lax.rem(my_core + lax.div(a, count_x) + t, count_core)
        z = lax.rem(my_z + t * 3, count_z)
        x = lax.rem(my_x + a + t, count_x)
        return (x * count_z + z) * count_core + core

    barrier = pltpu.get_barrier_semaphore()

    @pl.loop(1, count)
    def _(t):
        pl.semaphore_signal(barrier, inc=1, device_id=(target(t), blk), device_id_type=MESH)

    for peer in [(blk + d) % n_blk for d in range(1, n_blk)]:
        pl.semaphore_signal(barrier, inc=1, device_id=(leaf, peer), device_id_type=MESH)

    own = slot_ref[...]
    bits = lambda n: n.bit_length() - 1
    goal = own >> bits(points * n_blk)
    dc = ((goal & (count_core - 1)) - my_core) & (count_core - 1)
    dz = (((goal >> bits(count_core)) & (count_z - 1)) - my_z) & (count_z - 1)
    dx = ((goal >> bits(count_core * count_z)) - my_x) & (count_x - 1)
    turn = (dz * 3) & (count_z - 1)
    a = ((dx - turn) & (count_x - 1)) + count_x * ((dc - turn) & (count_core - 1))
    shift = chunk * (turn + count_z * a - goal)
    own_row = own.astype(f32)
    own_col = jnp.transpose(jnp.broadcast_to(own_row, (128, points)))
    at = lax.broadcasted_iota(jnp.int32, (points, 128), 0)
    for c in range(points // 128):
        lanes = slice(128 * c, 128 * c + 128)
        place = jnp.sum(jnp.where(own_col < own_row[:, lanes], 1.0, 0.0), axis=0, keepdims=True).astype(jnp.int32)
        hot[:, lanes] = jnp.where(at == place + shift[:, lanes], 1.0, 0.0).astype(bf16)

    fh, fl = halves(jnp.concatenate([feat_ref[...]] * 2, axis=0))
    ph, pl_low = halves(jnp.broadcast_to((own & (points - 1)).astype(f32), (16, points)))
    first = lax.broadcasted_iota(jnp.int32, (in_strip, chunk // 2, 2 * feats), 2) < feats
    oh, ol = halves(omega_ref[...])

    pairs = ((out_a, in_a), (out_s, in_s), (out_p, in_p))

    def moves(t, which):
        src, dst = pairs[which]
        return pltpu.make_async_remote_copy(
            src_ref=src.at[pl.ds(lax.div(t, in_strip) if which == 2 else t, 1)], dst_ref=dst.at[pl.ds(t, 1)],
            send_sem=send_sem.at[which], recv_sem=recv_sem.at[which, lax.div(t, per)],
            device_id=(target(t), blk), device_id_type=MESH)

    def whole(begin, end, which, g):
        into = pairs[which][1].at[pl.ds(begin, end - begin)]
        return pltpu.make_async_remote_copy(
            src_ref=into, dst_ref=into, send_sem=send_sem.at[which], recv_sem=recv_sem.at[which, g],
            device_id=(target(1), blk), device_id_type=MESH)

    def arrived(g, which):
        return whole(max(1, g * per), (g + 1) * per, which, g)

    for r in range(points // strip):
        h = hot[strip * r:strip * r + strip, :]
        lots = slice(in_strip * r, in_strip * r + in_strip)
        value = mm(h, oh, NT) + mm(h, ol, NT)
        for n in range(rank // 128):
            out_a[lots, chunk * n:chunk * n + chunk, :] = jnp.reshape(
                value[:, 128 * n:128 * n + 128], (in_strip, chunk, 128))
        value = jnp.reshape(mm(h, fh, NT) + mm(h, fl, NT), (in_strip, chunk, 2 * feats))
        out_a[lots, low:, 0:2 * feats] = jnp.where(first, value[:, :chunk // 2], value[:, chunk // 2:])
        out_p[r] = (mm(ph, h, NT) + mm(pl_low, h, NT))[0:1]
        if r == 0:
            pl.semaphore_wait(barrier, count - 1 + n_blk - 1)

        @pl.loop(max(1, in_strip * r), in_strip * r + in_strip)
        def _(t):
            moves(t, 0).start()

    sh, sl = halves(sketch_ref[...])
    for r in range(points // strip):
        h = hot[strip * r:strip * r + strip, :]
        out_s[in_strip * r:in_strip * r + in_strip] = jnp.reshape(
            mm(h, sh, NT) + mm(h, sl, NT), (in_strip, chunk, rank))

        @pl.loop(max(1, in_strip * r), in_strip * r + in_strip)
        def _(t):
            moves(t, 1).start()

    @pl.loop(1, count)
    def _(t):
        moves(t, 2).start()

    in_a[0] = out_a[0]
    in_s[0] = out_s[0]
    in_p[0] = out_p[0]

    def own_side(g, way):
        peer, slot_at = ((right, 0), (left, 1))[way]
        rows = pl.ds(g * per, per)
        return pltpu.make_async_remote_copy(
            src_ref=in_a.at[rows], dst_ref=side.at[slot_at, rows], send_sem=side_send.at[way, g],
            recv_sem=side_recv.at[slot_at, g], device_id=(leaf, peer), device_id_type=MESH)

    def relay(g, way):
        peer = (right, left)[way]
        rows = pl.ds((2 * g + way) * (per // 2), per // 2)
        return pltpu.make_async_remote_copy(
            src_ref=side.at[way, rows], dst_ref=side.at[2, rows], send_sem=side_send.at[2 + way, g],
            recv_sem=side_recv.at[2 + way, g], device_id=(leaf, peer), device_id_type=MESH)

    scale = -2.0 / feats * math.log2(math.e)

    def feats_of(lots):
        cut = lots[:, low:, 0:2 * feats]
        return jnp.reshape(jnp.concatenate([cut[:, :, :feats], cut[:, :, feats:]], axis=1), (wide, feats))

    def omegas_of(lots):
        return jnp.concatenate([jnp.reshape(lots[:, chunk * n:chunk * n + chunk], (wide, 128))
                                for n in range(rank // 128)], axis=1)

    one = jnp.ones((wide, 1), bf16)
    fill = jnp.zeros((wide, 256 - 3 * feats - 6), bf16)

    def arrive(g):
        arrived(g, 0).wait_recv()
        for way in range(2):
            own_side(g, way).start()
        x = feats_of(in_a[g * per:g * per + per])
        norm = thirds(jnp.sum(x * x, axis=1, keepdims=True) * scale)
        xh, xl = halves(x * (-2.0 * scale))
        row_aug[g * wide:g * wide + wide, :] = jnp.concatenate([xh, xh, xl, *norm, one, one, one, fill], axis=1)

    def hand_on(g):
        for way in range(2):
            own_side(g, way).wait_recv()
            relay(g, way).start()

    def absorb(block):
        x = feats_of(block)
        xh, xl = halves(x)
        norm = thirds(jnp.sum(x * x, axis=1, keepdims=True) * scale)
        col_aug = jnp.concatenate([xh, xl, xh, one, one, one, *norm, fill], axis=1)
        om = halves(omegas_of(block))
        for a in range(groups):
            rows = slice(a * wide, a * wide + wide)
            value = jnp.exp2(mm(row_aug[rows, :], col_aug, NT))
            acc[rows, :] += dot3(halves(value), om, NN)

    arrive(0)
    for g in range(1, groups):
        arrive(g)
        hand_on(g - 1)
    acc[...] = jnp.zeros_like(acc)

    @pl.loop(0, groups)
    def _(g):
        absorb(in_a[pl.ds(g * per, per)])

    hand_on(groups - 1)

    @pl.loop(0, 2 * groups)
    def _(i):
        absorb(side[lax.div(i, groups), pl.ds(lax.rem(i, groups) * per, per)])

    @pl.loop(0, groups)
    def _(g):
        for way in range(2):
            relay(g, way).wait_recv()
        absorb(side[2, pl.ds(g * per, per)])

    for g in range(groups):
        arrived(g, 1).wait_recv()
        rows = slice(g * wide, g * wide + wide)
        off = halves(jnp.reshape(in_s[g * per:g * per + per], (wide, rank)) - acc[rows, :])
        off_hi[rows, :], off_lo[rows, :] = off
        term = dot3(off, off, TN)
        if g == 0:
            gram[...] = term
        else:
            gram[...] += term

    steps = sum_subtrees(gram, leaf, blk, sums_ref, flat, part, run, got, stage, full, sum_sems)
    next(steps)
    for g in range(groups):
        arrived(g, 2).wait_recv()
    sub = lax.broadcasted_iota(jnp.int32, (in_strip, 1, strip), 0)
    lane = lax.broadcasted_iota(jnp.int32, (in_strip, 1, strip), 2)
    down = lax.broadcasted_iota(jnp.int32, (points, strip), 0)
    for u in range(points // strip):
        mine = jnp.where(lane // chunk == sub, in_p[u * in_strip:(u + 1) * in_strip], 0.0)
        row = jnp.sum(mine, axis=0).astype(jnp.int32)
        back[:, u * strip:(u + 1) * strip] = jnp.where(down == row, 1.0, 0.0).astype(bf16)
    for r in range(groups):
        rows = slice(r * wide, r * wide + wide)
        rhs_ref[rows, :] = mm(back[rows, :], off_hi[...], NN) + mm(back[rows, :], off_lo[...], NN)
    for _ in steps:
        pass

    for which in range(3):
        whole(1, count, which, 0).wait_send()

    @pl.loop(0, groups)
    def _(g):
        for way in range(2):
            own_side(g, way).wait_send()
            relay(g, way).wait_send()


def near_field(slot, features, sketch, omega, depth):
    feats, points = features.shape
    rank = sketch.shape[0]
    count = lax.axis_size("leaf")
    n_blk = lax.axis_size("blk")
    core = 2
    z = min(8, count // core)
    dims = (count // (core * z), z, core)
    half = rank // 2
    lines = 3 * half
    piece = lines // n_blk
    rounds = depth // 2
    chunk = points // count
    lot = rank // 128 * chunk + chunk // 2
    strip = min(128, points // 4)
    vm = lambda *shape: pltpu.VMEM(shape, f32)
    vb = lambda *shape: pltpu.VMEM(shape, bf16)
    dma = lambda *shape: pltpu.SemaphoreType.DMA(shape)
    return pl.pallas_call(
        functools.partial(near_kernel, dims),
        out_shape=(jax.ShapeDtypeStruct((depth + 1, lines, half), f32), jax.ShapeDtypeStruct((points, rank), f32)),
        in_specs=[pl.BlockSpec(memory_space=pltpu.VMEM)] * 4,
        out_specs=[pl.BlockSpec(memory_space=pltpu.VMEM)] * 2,
        scratch_shapes=[
            vb(points, points), vb(points, points),
            vm(count, lot, 128), vm(points // strip, 1, strip), vm(count, chunk, rank),
            vm(count, lot, 128), vm(count, 1, strip), vm(count, chunk, rank),
            vm(3, count, lot, 128), vm(points, rank), vb(points, 256), vm(rank, rank),
            vb(points, rank), vb(points, rank),
            vm(lines, half), vm(n_blk - 1, piece, half), vm(rounds, piece, half), vm(rounds, 3, piece, half),
            vm(depth + 1, piece, half), vm(depth + 1, lines, half),
            dma(3), dma(3, 4), dma(4, 4), dma(4, 4),
            dma(n_blk - 1), dma(n_blk - 1), dma(rounds, 3), dma(rounds, 3),
            dma(rounds + 1, n_blk - 1), dma(rounds + 1, n_blk - 1),
        ],
        compiler_params=pltpu.CompilerParams(collective_id=0, has_side_effects=True, vmem_limit_bytes=56 << 20),
    )(slot[None], features, sketch, omega)


def per_device(features, sketch, omega, slot, column_order):
    depth = column_order.shape[0]
    sums, turned = near_field(slot, features, sketch, omega, depth)
    second = lax.axis_index("leaf") >> jnp.arange(depth, dtype=jnp.int32) & 1
    leaf_basis, transfers = tri(column_order, sums, second, turned)
    return (leaf_basis, transfers[None])


def solution(mesh):
    placed = (
        P(None, ("leaf", "blk")),
        P(None, ("leaf", "blk")),
        P(None, ("leaf", "blk")),
        P(("leaf", "blk")),
        P(),
    )
    return jax.shard_map(
        per_device,
        mesh=mesh,
        in_specs=placed,
        out_specs=(P(None, ("leaf", "blk")), P("leaf", None, None, None)),
        check_vma=False,
    )
```

```python
import functools
import math

import jax
import jax.numpy as jnp
from jax import lax
from jax.experimental import pallas as pl
from jax.experimental.pallas import tpu as pltpu
from jax.sharding import PartitionSpec as P

NN = (((1,), (0,)), ((), ()))
NT = (((1,), (1,)), ((), ()))
TN = (((0,), (0,)), ((), ()))
f32, bf16 = jnp.float32, jnp.bfloat16


def mm(a, b, dims):
    return lax.dot_general(a, b, dims, preferred_element_type=f32)


def halves(x):
    hi = x.astype(bf16)
    return hi, (x - hi.astype(f32)).astype(bf16)


def thirds(x):
    hi = x.astype(bf16)
    rest = x - hi.astype(f32)
    mid = rest.astype(bf16)
    return hi, mid, (rest - mid.astype(f32)).astype(bf16)


def dot3(a, b, dims):
    return mm(a[0], b[0], dims) + (mm(a[0], b[1], dims) + mm(a[1], b[0], dims))


def dotf(a, b, dims):
    return dot3(halves(a), halves(b), dims)


def pick(x, hot, dims, left):
    hi, lo = halves(x)
    if left:
        return mm(hi, hot, dims) + mm(lo, hot, dims)
    return mm(hot, hi, dims) + mm(hot, lo, dims)


NB = 32
TILE = 8


def spread_row(x, i):
    return jnp.broadcast_to(x[i:i + 1, :], x.shape)


def diag_inverses(blocks):
    tiles = NB // TILE
    width = 128 * len(blocks)
    a = [jnp.concatenate([x[TILE * q:TILE * q + TILE] for x in blocks], axis=1) for q in range(tiles)]
    lane = lax.broadcasted_iota(jnp.int32, (TILE, width), 1) % NB
    row = lax.broadcasted_iota(jnp.int32, (TILE, width), 0)
    base = lax.broadcasted_iota(jnp.int32, (TILE, 128), 1) // NB * NB
    b = [jnp.where(lane == row + TILE * q, 1.0, 0.0).astype(f32) for q in range(tiles)]

    def column(x, k):
        return jnp.concatenate(
            [jnp.take_along_axis(x[:, 128 * g:128 * g + 128], base + k, axis=1, mode="promise_in_bounds")
             for g in range(len(blocks))], axis=1)

    done = []
    for p in range(tiles):
        below = range(p, tiles)
        cols = [{q: column(a[q], TILE * p + i) for q in below} for i in range(TILE)]
        mult = []
        scale = jnp.zeros((TILE, width), f32)
        for i in range(TILE):
            root = lax.rsqrt(spread_row(cols[i][p], i))
            scale = jnp.where(row == i, root, scale)
            m = {q: cols[i][q] * (root * root) for q in below}
            m[p] = jnp.where(row > i, m[p], 0.0)
            mult.append(m)
            for t in range(i + 1, TILE):
                head = spread_row(cols[t][p], i)
                for q in below:
                    cols[t][q] = cols[t][q] - m[q] * head
            if i + 1 < TILE:
                a[p] = a[p] - m[p] * spread_row(a[p], i)
                b[p] = b[p] - m[p] * spread_row(b[p], i)
        for i in range(TILE):
            ra, rb = spread_row(a[p], i), spread_row(b[p], i)
            for q in range(p + 1, tiles):
                a[q] = a[q] - mult[i][q] * ra
                b[q] = b[q] - mult[i][q] * rb
        done.append(b[p] * scale)
    whole = jnp.concatenate(done, axis=0)
    return [whole[:, 128 * g:128 * g + 128] for g in range(len(blocks))]


def tri_kernel(n_inv_groups, order_ref, gram_ref, second_ref, rhs_ref, basis_ref, trans_ref,
               own, sib, panel, inv, fact, finv, rhs_in, basis_out, trans_out, load_sem, store_sem):
    groups = 4
    load = pltpu.make_async_copy(rhs_ref, rhs_in, load_sem)
    load.start()
    size = order_ref.shape[1]
    half = size // 2
    steps = size // NB
    depth = order_ref.shape[0]
    slots = 2 * depth + 1
    isub = lax.broadcasted_iota(jnp.int32, (size, size), 0)
    hot = [jnp.where(isub == order_ref[l:l + 1, :], 1.0, 0.0).astype(bf16) for l in range(depth)]
    total = [hot[0]]
    for l in range(1, depth):
        total.append(mm(total[-1], hot[l], NN).astype(bf16))

    def reorder(g, q):
        return pick(pick(g, q, NN, True), q, TN, False)

    def unfold(at):
        low = gram_ref[at, half:2 * half, :]
        top = jnp.concatenate([gram_ref[at, 0:half, :], jnp.transpose(low)], axis=1)
        return jnp.concatenate([top, jnp.concatenate([low, gram_ref[at, 2 * half:, :]], axis=1)], axis=0)

    running = unfold(0)
    own[0] = running
    for l in range(depth):
        g = unfold(l + 1)
        sib[l] = g if l == 0 else reorder(g, total[l - 1])
        running = running + g
        own[l + 1] = reorder(running, total[l])

    def dense(s):
        if s <= depth:
            return own, s
        return sib, min(s - depth - 1, depth - 1)

    for j in range(steps):
        for g in range(groups):
            lo = NB * j
            pieces = []
            for t in range(4):
                ref, at = dense(min(4 * g + t, slots - 1))
                pieces.append(ref[at, lo:lo + NB, lo // 128 * 128:])
            panel[g, j, lo // 128 * 128:, :] = jnp.concatenate(pieces, axis=0).T

    lane = lax.broadcasted_iota(jnp.int32, (NB, 128), 1)
    rows = lax.broadcasted_iota(jnp.int32, (NB, 128), 0)
    seg_base = (lane // NB) * NB
    r128 = lax.broadcasted_iota(jnp.int32, (128, 128), 0) // NB
    l128 = lax.broadcasted_iota(jnp.int32, (128, 128), 1) // NB
    same = r128 == l128

    same = jnp.where(same, 1.0, 0.0).astype(bf16)

    def spread(x):
        return [jnp.concatenate([part] * 4, axis=0) * same for part in halves(x)]

    def spread_all(blocks, axis):
        return [jnp.concatenate(parts, axis=axis) for parts in zip(*[spread(x) for x in blocks])]

    for j in range(steps):
        lo = NB * j
        nxt = lo + NB
        inverses = diag_inverses([panel[g, j, lo:nxt, :] for g in range(groups)])
        for g in range(groups):
            li = inverses[g]
            lp = dot3(halves(panel[g, j, lo:, :]), spread(li), NT)
            top = jnp.where(lane - seg_base <= rows, lp[:NB], 0.0)
            if lo % 128:
                panel[g, j, lo // 128 * 128:lo, :] = jnp.zeros((lo % 128, 128), f32)
            panel[g, j, lo:nxt, :] = top
            if nxt < size:
                panel[g, j, nxt:, :] = lp[NB:]
                low = lp[NB:]
                lowh = halves(low)
                for i in range(j + 1, steps, 2):
                    at = NB * (i - j - 1)
                    pair = range(i, min(i + 2, steps))
                    rhs = spread_all([low[NB * (k - j - 1):NB * (k - j)] for k in pair], 0)
                    upd = dot3((lowh[0][at:], lowh[1][at:]), rhs, NT)
                    for n, k in enumerate(pair):
                        panel[g, k, NB * k:, :] -= upd[NB * n:, 128 * n:128 * n + 128]
            if g < n_inv_groups:
                lih = halves(li)
                for c in range(0, j + 1, 2):
                    pair = [k for k in (c, c + 1) if k < j]
                    xs = []
                    if pair:
                        prod = dot3(lih, spread_all([inv[g, k, lo:nxt, :] for k in pair], 1), NN)
                        xs = [prod[:, 128 * n:128 * n + 128] for n in range(len(pair))]
                    if c + len(pair) == j and len(pair) < 2:
                        pair.append(j)
                        xs.append(li)
                    for k, x in zip(pair, xs):
                        inv[g, k, lo:nxt, :] = x
                    if nxt < size:
                        upd = dot3(lowh, spread_all(xs, 1), NN)
                        for n, k in enumerate(pair):
                            piece = upd[:, 128 * n:128 * n + 128]
                            if k == j:
                                inv[g, k, nxt:, :] = -piece
                            else:
                                inv[g, k, nxt:, :] -= piece
                if lo % 128:
                    inv[g, j, lo // 128 * 128:lo, :] = jnp.zeros((lo % 128, 128), f32)

    def unpack(source, into, g, last):
        for j in range(steps):
            begin = NB * j // 128 * 128
            flat = source[g, j, begin:, :].T
            for t in range(4):
                at = 4 * g + t
                if at < last:
                    if begin:
                        into[at, NB * j:NB * j + NB, :begin] = jnp.zeros((NB, begin), f32)
                    into[at, NB * j:NB * j + NB, begin:] = flat[NB * t:NB * t + NB]

    for g in range(n_inv_groups):
        unpack(inv, finv, g, depth + 1)

    stores = []

    def store(src, dst):
        stores.append(pltpu.make_async_copy(src, dst, store_sem.at[len(stores)]))
        stores[-1].start()

    load.wait()
    inverse = jnp.transpose(finv[0]) * math.sqrt(rhs_ref.shape[0] * lax.axis_size("blk"))
    basis_out[...] = dotf(inverse, rhs_in[...], NT)
    store(basis_out, basis_ref)
    for g in range(groups):
        unpack(panel, fact, g, slots)
    for l in range(depth):
        v = halves(pick(finv[l + 1] * math.sqrt(2 * size), hot[l], NN, False))
        second = second_ref[l]
        trans_out[l, pl.ds(pl.multiple_of(second * size, size), size), :] = dot3(halves(fact[l]), v, NN)
        trans_out[l, pl.ds(pl.multiple_of((1 - second) * size, size), size), :] = dot3(
            halves(fact[depth + 1 + l]), v, NN)
        store(trans_out.at[l], trans_ref.at[l])
    for copy in stores:
        copy.wait()


def tri(order, grams, second, rhs):
    depth, size = order.shape
    return pl.pallas_call(
        functools.partial(tri_kernel, 2),
        out_shape=(jax.ShapeDtypeStruct(rhs.shape[::-1], f32), jax.ShapeDtypeStruct((depth, 2 * size, size), f32)),
        in_specs=[pl.BlockSpec(memory_space=pltpu.VMEM), pl.BlockSpec(memory_space=pltpu.VMEM),
                  pl.BlockSpec(memory_space=pltpu.SMEM), pl.BlockSpec(memory_space=pl.ANY)],
        out_specs=[pl.BlockSpec(memory_space=pl.ANY)] * 2,
        scratch_shapes=[
            pltpu.VMEM((depth + 1, size, size), f32),
            pltpu.VMEM((depth, size, size), f32),
            pltpu.VMEM((4, 8, size, 128), f32),
            pltpu.VMEM((2, 8, size, 128), f32),
            pltpu.VMEM((2 * depth + 1, size, size), f32),
            pltpu.VMEM((depth + 1, size, size), f32),
            pltpu.VMEM(rhs.shape, f32),
            pltpu.VMEM(rhs.shape[::-1], f32),
            pltpu.VMEM((depth, 2 * size, size), f32),
            pltpu.SemaphoreType.DMA,
            pltpu.SemaphoreType.DMA((depth + 1,)),
        ],
        compiler_params=pltpu.CompilerParams(vmem_limit_bytes=48 << 20),
    )(order, grams, second, rhs)


MESH = pl.DeviceIdType.MESH


def sum_subtrees(gram, leaf, blk, out_ref, flat, part, run, got, stage, full, sems):
    part_send, part_recv, got_send, got_recv, fwd_send, fwd_recv = sems
    n_blk = lax.axis_size("blk")
    rounds = run.shape[0]
    half = flat.shape[1]
    piece = run.shape[1]

    def mates(r):
        unit = 4 ** r
        digit = (leaf // unit) % 4
        moved = (digit + 1 - 2 * (digit % 2), digit + 2 - 4 * (digit // 2), 3 - digit)
        return [leaf + (m - digit) * unit for m in moved]

    flat[0:half] = gram[0:half, 0:half]
    flat[half:2 * half] = gram[half:, 0:half]
    flat[2 * half:] = gram[half:, half:]
    started = []

    def send(src, dst, s_sem, r_sem, device):
        copy = pltpu.make_async_remote_copy(src_ref=src, dst_ref=dst, send_sem=s_sem, recv_sem=r_sem,
                                            device_id=device, device_id_type=MESH)
        copy.start()
        started.append(copy)
        return copy

    first = []
    for d in range(1, n_blk):
        peer = (blk + d) % n_blk
        first.append(send(flat.at[pl.ds(pl.multiple_of(peer * piece, 8), piece)], part.at[d - 1],
                          part_send.at[d - 1], part_recv.at[d - 1], (leaf, peer)))
    yield
    mine = pl.multiple_of(blk * piece, 8)
    forwards = []

    def forward(slot_at, begin, size):
        for d in range(1, n_blk):
            forwards.append(send(stage.at[pl.ds(begin, size)], full.at[pl.ds(begin, size), pl.ds(mine, piece)],
                                 fwd_send.at[slot_at, d - 1], fwd_recv.at[slot_at, d - 1], (leaf, (blk + d) % n_blk)))

    for copy in first:
        copy.wait_recv()
    run[0] = flat[pl.ds(mine, piece)] + ((part[0] + part[1]) + part[2])
    for r in range(rounds):
        copies = [send(run.at[r], got.at[r, m], got_send.at[r, m], got_recv.at[r, m], (mate, blk))
                  for m, mate in enumerate(mates(r))]
        if r == 0:
            stage[0] = run[0]
            full[0, pl.ds(mine, piece)] = stage[0]
            forward(0, 0, 1)
        else:
            forward(r, 2 * r - 1, 2)
        for copy in copies:
            copy.wait_recv()
        near = got[r, 0]
        far = got[r, 1] + got[r, 2]
        if r + 1 < rounds:
            run[r + 1] = run[r] + near + far
        for k, value in enumerate((near, far)):
            stage[1 + 2 * r + k] = value
            full[1 + 2 * r + k, pl.ds(mine, piece)] = value
    forward(rounds, 2 * rounds - 1, 2)
    for copy in forwards:
        copy.wait_recv()
    for copy in started:
        copy.wait_send()
    out_ref[...] = full[...]


def near_kernel(dims, slot_ref, feat_ref, sketch_ref, omega_ref, sums_ref, rhs_ref,
                hot, back, out_a, out_p, out_s, in_a, in_p, in_s, side, acc, row_aug, gram, off_hi, off_lo,
                flat, part, run, got, stage, full,
                omega_in, sketch_in, load_sem, send_sem, recv_sem, side_send, side_recv, *sum_sems):
    count_x, count_z, count_core = dims
    count = count_x * count_z * count_core
    leaf, blk = lax.axis_index("leaf"), lax.axis_index("blk")
    n_blk = lax.axis_size("blk")
    points = slot_ref.shape[1]
    chunk = points // count
    feats = feat_ref.shape[0]
    groups = 4
    per = count // groups
    rank = omega_ref.shape[0]
    lot = out_a.shape[1]
    low = lot - chunk // 2
    wide = points // groups
    strip = min(128, wide)
    in_strip = strip // chunk
    my_core = leaf % count_core
    my_z = (leaf // count_core) % count_z
    my_x = leaf // (count_core * count_z)
    right, left = (blk + 1) % n_blk, (blk + n_blk - 1) % n_blk

    def target(t):
        a = lax.div(t, count_z)
        core = lax.rem(my_core + lax.div(a, count_x) + t, count_core)
        z = lax.rem(my_z + t * 3, count_z)
        x = lax.rem(my_x + a + t, count_x)
        return (x * count_z + z) * count_core + core

    load_omega = pltpu.make_async_copy(omega_ref, omega_in, load_sem.at[0])
    load_sketch = pltpu.make_async_copy(sketch_ref, sketch_in, load_sem.at[1])
    load_omega.start()
    load_sketch.start()
    barrier = pltpu.get_barrier_semaphore()

    @pl.loop(1, count)
    def _(t):
        pl.semaphore_signal(barrier, inc=1, device_id=(target(t), blk), device_id_type=MESH)

    for peer in [(blk + d) % n_blk for d in range(1, n_blk)]:
        pl.semaphore_signal(barrier, inc=1, device_id=(leaf, peer), device_id_type=MESH)

    own = slot_ref[...]
    bits = lambda n: n.bit_length() - 1
    goal = own >> bits(points * n_blk)
    dc = ((goal & (count_core - 1)) - my_core) & (count_core - 1)
    dz = (((goal >> bits(count_core)) & (count_z - 1)) - my_z) & (count_z - 1)
    dx = ((goal >> bits(count_core * count_z)) - my_x) & (count_x - 1)
    turn = (dz * 3) & (count_z - 1)
    a = ((dx - turn) & (count_x - 1)) + count_x * ((dc - turn) & (count_core - 1))
    shift = chunk * (turn + count_z * a - goal)
    own_row = own.astype(f32)
    own_col = jnp.transpose(jnp.broadcast_to(own_row, (128, points)))
    at = lax.broadcasted_iota(jnp.int32, (points, 128), 0)
    for c in range(points // 128):
        lanes = slice(128 * c, 128 * c + 128)
        place = jnp.sum(jnp.where(own_col < own_row[:, lanes], 1.0, 0.0), axis=0, keepdims=True).astype(jnp.int32)
        hot[:, lanes] = jnp.where(at == place + shift[:, lanes], 1.0, 0.0).astype(bf16)

    fh, fl = halves(jnp.concatenate([feat_ref[...]] * 2, axis=0))
    ph, pl_low = halves(jnp.broadcast_to((own & (points - 1)).astype(f32), (16, points)))
    first = lax.broadcasted_iota(jnp.int32, (in_strip, chunk // 2, 2 * feats), 2) < feats
    load_omega.wait()
    oh, ol = halves(omega_in[...])

    pairs = ((out_a, in_a), (out_s, in_s), (out_p, in_p))

    def moves(t, which):
        src, dst = pairs[which]
        return pltpu.make_async_remote_copy(
            src_ref=src.at[pl.ds(lax.div(t, in_strip) if which == 2 else t, 1)], dst_ref=dst.at[pl.ds(t, 1)],
            send_sem=send_sem.at[which], recv_sem=recv_sem.at[which, lax.div(t, per)],
            device_id=(target(t), blk), device_id_type=MESH)

    def whole(begin, end, which, g):
        into = pairs[which][1].at[pl.ds(begin, end - begin)]
        return pltpu.make_async_remote_copy(
            src_ref=into, dst_ref=into, send_sem=send_sem.at[which], recv_sem=recv_sem.at[which, g],
            device_id=(target(1), blk), device_id_type=MESH)

    def arrived(g, which):
        return whole(max(1, g * per), (g + 1) * per, which, g)

    for r in range(points // strip):
        h = hot[strip * r:strip * r + strip, :]
        lots = slice(in_strip * r, in_strip * r + in_strip)
        value = mm(h, oh, NT) + mm(h, ol, NT)
        for n in range(rank // 128):
            out_a[lots, chunk * n:chunk * n + chunk, :] = jnp.reshape(
                value[:, 128 * n:128 * n + 128], (in_strip, chunk, 128))
        value = jnp.reshape(mm(h, fh, NT) + mm(h, fl, NT), (in_strip, chunk, 2 * feats))
        out_a[lots, low:, 0:2 * feats] = jnp.where(first, value[:, :chunk // 2], value[:, chunk // 2:])
        out_p[r] = (mm(ph, h, NT) + mm(pl_low, h, NT))[0:1]
        if r == 0:
            pl.semaphore_wait(barrier, count - 1 + n_blk - 1)

        @pl.loop(max(1, in_strip * r), in_strip * r + in_strip)
        def _(t):
            moves(t, 0).start()

    load_sketch.wait()
    sh, sl = halves(sketch_in[...])
    for r in range(points // strip):
        h = hot[strip * r:strip * r + strip, :]
        out_s[in_strip * r:in_strip * r + in_strip] = jnp.reshape(
            mm(h, sh, NT) + mm(h, sl, NT), (in_strip, chunk, rank))

        @pl.loop(max(1, in_strip * r), in_strip * r + in_strip)
        def _(t):
            moves(t, 1).start()

    @pl.loop(1, count)
    def _(t):
        moves(t, 2).start()

    in_a[0] = out_a[0]
    in_s[0] = out_s[0]
    in_p[0] = out_p[0]

    def own_side(g, way):
        peer, slot_at = ((right, 0), (left, 1))[way]
        rows = pl.ds(g * per, per)
        return pltpu.make_async_remote_copy(
            src_ref=in_a.at[rows], dst_ref=side.at[slot_at, rows], send_sem=side_send.at[way, g],
            recv_sem=side_recv.at[slot_at, g], device_id=(leaf, peer), device_id_type=MESH)

    def relay(g, way):
        peer = (right, left)[way]
        rows = pl.ds((2 * g + way) * (per // 2), per // 2)
        return pltpu.make_async_remote_copy(
            src_ref=side.at[way, rows], dst_ref=side.at[2, rows], send_sem=side_send.at[2 + way, g],
            recv_sem=side_recv.at[2 + way, g], device_id=(leaf, peer), device_id_type=MESH)

    scale = -2.0 / feats * math.log2(math.e)

    def feats_of(lots):
        cut = lots[:, low:, 0:2 * feats]
        return jnp.reshape(jnp.concatenate([cut[:, :, :feats], cut[:, :, feats:]], axis=1), (wide, feats))

    def omegas_of(lots):
        return jnp.concatenate([jnp.reshape(lots[:, chunk * n:chunk * n + chunk], (wide, 128))
                                for n in range(rank // 128)], axis=1)

    one = jnp.ones((wide, 1), bf16)
    fill = jnp.zeros((wide, 256 - 3 * feats - 6), bf16)

    def arrive(g):
        arrived(g, 0).wait_recv()
        for way in range(2):
            own_side(g, way).start()
        x = feats_of(in_a[g * per:g * per + per])
        norm = thirds(jnp.sum(x * x, axis=1, keepdims=True) * scale)
        xh, xl = halves(x * (-2.0 * scale))
        row_aug[g * wide:g * wide + wide, :] = jnp.concatenate([xh, xh, xl, *norm, one, one, one, fill], axis=1)

    def hand_on(g):
        for way in range(2):
            own_side(g, way).wait_recv()
            relay(g, way).start()

    def absorb(block):
        x = feats_of(block)
        xh, xl = halves(x)
        norm = thirds(jnp.sum(x * x, axis=1, keepdims=True) * scale)
        col_aug = jnp.concatenate([xh, xl, xh, one, one, one, *norm, fill], axis=1)
        om = halves(omegas_of(block))
        for a in range(groups):
            rows = slice(a * wide, a * wide + wide)
            value = jnp.exp2(mm(row_aug[rows, :], col_aug, NT))
            acc[rows, :] += dot3(halves(value), om, NN)

    arrive(0)
    for g in range(1, groups):
        arrive(g)
        hand_on(g - 1)
    acc[...] = jnp.zeros_like(acc)

    @pl.loop(0, groups)
    def _(g):
        absorb(in_a[pl.ds(g * per, per)])

    hand_on(groups - 1)

    @pl.loop(0, 2 * groups)
    def _(i):
        absorb(side[lax.div(i, groups), pl.ds(lax.rem(i, groups) * per, per)])

    @pl.loop(0, groups)
    def _(g):
        for way in range(2):
            relay(g, way).wait_recv()
        absorb(side[2, pl.ds(g * per, per)])

    for g in range(groups):
        arrived(g, 1).wait_recv()
        rows = slice(g * wide, g * wide + wide)
        off = halves(jnp.reshape(in_s[g * per:g * per + per], (wide, rank)) - acc[rows, :])
        off_hi[rows, :], off_lo[rows, :] = off
        term = dot3(off, off, TN)
        if g == 0:
            gram[...] = term
        else:
            gram[...] += term

    steps = sum_subtrees(gram, leaf, blk, sums_ref, flat, part, run, got, stage, full, sum_sems)
    next(steps)
    for g in range(groups):
        arrived(g, 2).wait_recv()
    sub = lax.broadcasted_iota(jnp.int32, (in_strip, 1, strip), 0)
    lane = lax.broadcasted_iota(jnp.int32, (in_strip, 1, strip), 2)
    down = lax.broadcasted_iota(jnp.int32, (points, strip), 0)
    for u in range(points // strip):
        mine = jnp.where(lane // chunk == sub, in_p[u * in_strip:(u + 1) * in_strip], 0.0)
        row = jnp.sum(mine, axis=0).astype(jnp.int32)
        back[:, u * strip:(u + 1) * strip] = jnp.where(down == row, 1.0, 0.0).astype(bf16)
    for r in range(groups):
        rows = slice(r * wide, r * wide + wide)
        rhs_ref[rows, :] = mm(back[rows, :], off_hi[...], NN) + mm(back[rows, :], off_lo[...], NN)
    for _ in steps:
        pass

    for which in range(3):
        whole(1, count, which, 0).wait_send()

    @pl.loop(0, groups)
    def _(g):
        for way in range(2):
            own_side(g, way).wait_send()
            relay(g, way).wait_send()


def near_field(slot, features, sketch, omega, depth):
    feats, points = features.shape
    rank = sketch.shape[0]
    count = lax.axis_size("leaf")
    n_blk = lax.axis_size("blk")
    core = 2
    z = min(8, count // core)
    dims = (count // (core * z), z, core)
    half = rank // 2
    lines = 3 * half
    piece = lines // n_blk
    rounds = depth // 2
    chunk = points // count
    lot = rank // 128 * chunk + chunk // 2
    strip = min(128, points // 4)
    vm = lambda *shape: pltpu.VMEM(shape, f32)
    vb = lambda *shape: pltpu.VMEM(shape, bf16)
    dma = lambda *shape: pltpu.SemaphoreType.DMA(shape)
    return pl.pallas_call(
        functools.partial(near_kernel, dims),
        out_shape=(jax.ShapeDtypeStruct((depth + 1, lines, half), f32), jax.ShapeDtypeStruct((points, rank), f32)),
        in_specs=[pl.BlockSpec(memory_space=pltpu.VMEM)] * 2 + [pl.BlockSpec(memory_space=pl.ANY)] * 2,
        out_specs=[pl.BlockSpec(memory_space=pltpu.VMEM)] * 2,
        scratch_shapes=[
            vb(points, points), vb(points, points),
            vm(count, lot, 128), vm(points // strip, 1, strip), vm(count, chunk, rank),
            vm(count, lot, 128), vm(count, 1, strip), vm(count, chunk, rank),
            vm(3, count, lot, 128), vm(points, rank), vb(points, 256), vm(rank, rank),
            vb(points, rank), vb(points, rank),
            vm(lines, half), vm(n_blk - 1, piece, half), vm(rounds, piece, half), vm(rounds, 3, piece, half),
            vm(depth + 1, piece, half), vm(depth + 1, lines, half),
            vm(rank, points), vm(rank, points), dma(2), dma(3), dma(3, 4), dma(4, 4), dma(4, 4),
            dma(n_blk - 1), dma(n_blk - 1), dma(rounds, 3), dma(rounds, 3),
            dma(rounds + 1, n_blk - 1), dma(rounds + 1, n_blk - 1),
        ],
        compiler_params=pltpu.CompilerParams(collective_id=0, has_side_effects=True, vmem_limit_bytes=56 << 20),
    )(slot[None], features, sketch, omega)


def per_device(features, sketch, omega, slot, column_order):
    depth = column_order.shape[0]
    sums, turned = near_field(slot, features, sketch, omega, depth)
    second = lax.axis_index("leaf") >> jnp.arange(depth, dtype=jnp.int32) & 1
    leaf_basis, transfers = tri(column_order, sums, second, turned)
    return (leaf_basis, transfers[None])


def solution(mesh):
    placed = (
        P(None, ("leaf", "blk")),
        P(None, ("leaf", "blk")),
        P(None, ("leaf", "blk")),
        P(("leaf", "blk")),
        P(),
    )
    return jax.shard_map(
        per_device,
        mesh=mesh,
        in_specs=placed,
        out_specs=(P(None, ("leaf", "blk")), P("leaf", None, None, None)),
        check_vma=False,
    )
```

```python
import functools
import math

import jax
import jax.numpy as jnp
from jax import lax
from jax.experimental import pallas as pl
from jax.experimental.pallas import tpu as pltpu
from jax.sharding import PartitionSpec as P

NN = (((1,), (0,)), ((), ()))
NT = (((1,), (1,)), ((), ()))
TN = (((0,), (0,)), ((), ()))
f32, bf16 = jnp.float32, jnp.bfloat16


def mm(a, b, dims):
    return lax.dot_general(a, b, dims, preferred_element_type=f32)


def halves(x):
    hi = x.astype(bf16)
    return hi, (x - hi.astype(f32)).astype(bf16)


def thirds(x):
    hi = x.astype(bf16)
    rest = x - hi.astype(f32)
    mid = rest.astype(bf16)
    return hi, mid, (rest - mid.astype(f32)).astype(bf16)


def dot3(a, b, dims):
    return mm(a[0], b[0], dims) + (mm(a[0], b[1], dims) + mm(a[1], b[0], dims))


def dotf(a, b, dims):
    return dot3(halves(a), halves(b), dims)


def pick(x, hot, dims, left):
    hi, lo = halves(x)
    if left:
        return mm(hi, hot, dims) + mm(lo, hot, dims)
    return mm(hot, hi, dims) + mm(hot, lo, dims)


NB = 32
TILE = 8


def spread_row(x, i):
    return jnp.broadcast_to(x[i:i + 1, :], x.shape)


def diag_inverses(blocks):
    tiles = NB // TILE
    width = 128 * len(blocks)
    a = [jnp.concatenate([x[TILE * q:TILE * q + TILE] for x in blocks], axis=1) for q in range(tiles)]
    lane = lax.broadcasted_iota(jnp.int32, (TILE, width), 1) % NB
    row = lax.broadcasted_iota(jnp.int32, (TILE, width), 0)
    base = lax.broadcasted_iota(jnp.int32, (TILE, 128), 1) // NB * NB
    b = [jnp.where(lane == row + TILE * q, 1.0, 0.0).astype(f32) for q in range(tiles)]

    def column(x, k):
        return jnp.concatenate(
            [jnp.take_along_axis(x[:, 128 * g:128 * g + 128], base + k, axis=1, mode="promise_in_bounds")
             for g in range(len(blocks))], axis=1)

    done = []
    for p in range(tiles):
        below = range(p, tiles)
        cols = [{q: column(a[q], TILE * p + i) for q in below} for i in range(TILE)]
        mult = []
        scale = jnp.zeros((TILE, width), f32)
        for i in range(TILE):
            root = lax.rsqrt(spread_row(cols[i][p], i))
            scale = jnp.where(row == i, root, scale)
            m = {q: cols[i][q] * (root * root) for q in below}
            m[p] = jnp.where(row > i, m[p], 0.0)
            mult.append(m)
            for t in range(i + 1, TILE):
                head = spread_row(cols[t][p], i)
                for q in below:
                    cols[t][q] = cols[t][q] - m[q] * head
            if i + 1 < TILE:
                a[p] = a[p] - m[p] * spread_row(a[p], i)
                b[p] = b[p] - m[p] * spread_row(b[p], i)
        for i in range(TILE):
            ra, rb = spread_row(a[p], i), spread_row(b[p], i)
            for q in range(p + 1, tiles):
                a[q] = a[q] - mult[i][q] * ra
                b[q] = b[q] - mult[i][q] * rb
        done.append(b[p] * scale)
    whole = jnp.concatenate(done, axis=0)
    return [whole[:, 128 * g:128 * g + 128] for g in range(len(blocks))]


def tri_kernel(n_inv_groups, order_ref, gram_ref, second_ref, rhs_ref, basis_ref, trans_ref,
               own, sib, panel, inv, fact, finv, rhs_in, basis_out, trans_out, load_sem, store_sem):
    groups = 4
    load = pltpu.make_async_copy(rhs_ref, rhs_in, load_sem)
    load.start()
    size = order_ref.shape[1]
    half = size // 2
    steps = size // NB
    depth = order_ref.shape[0]
    slots = 2 * depth + 1
    isub = lax.broadcasted_iota(jnp.int32, (size, size), 0)
    hot = [jnp.where(isub == order_ref[l:l + 1, :], 1.0, 0.0).astype(bf16) for l in range(depth)]
    total = [hot[0]]
    for l in range(1, depth):
        total.append(mm(total[-1], hot[l], NN).astype(bf16))

    def reorder(g, q):
        return pick(pick(g, q, NN, True), q, TN, False)

    def unfold(at):
        low = gram_ref[at, half:2 * half, :]
        top = jnp.concatenate([gram_ref[at, 0:half, :], jnp.transpose(low)], axis=1)
        return jnp.concatenate([top, jnp.concatenate([low, gram_ref[at, 2 * half:, :]], axis=1)], axis=0)

    running = unfold(0)
    own[0] = running
    for l in range(depth):
        g = unfold(l + 1)
        sib[l] = g if l == 0 else reorder(g, total[l - 1])
        running = running + g
        own[l + 1] = reorder(running, total[l])

    def dense(s):
        if s <= depth:
            return own, s
        return sib, min(s - depth - 1, depth - 1)

    for j in range(steps):
        for g in range(groups):
            lo = NB * j
            pieces = []
            for t in range(4):
                ref, at = dense(min(4 * g + t, slots - 1))
                pieces.append(ref[at, lo:lo + NB, lo // 128 * 128:])
            panel[g, j, lo // 128 * 128:, :] = jnp.concatenate(pieces, axis=0).T

    lane = lax.broadcasted_iota(jnp.int32, (NB, 128), 1)
    rows = lax.broadcasted_iota(jnp.int32, (NB, 128), 0)
    seg_base = (lane // NB) * NB
    r128 = lax.broadcasted_iota(jnp.int32, (128, 128), 0) // NB
    l128 = lax.broadcasted_iota(jnp.int32, (128, 128), 1) // NB
    same = r128 == l128

    same = jnp.where(same, 1.0, 0.0).astype(bf16)

    def spread(x):
        return [jnp.concatenate([part] * 4, axis=0) * same for part in halves(x)]

    def spread_all(blocks, axis):
        return [jnp.concatenate(parts, axis=axis) for parts in zip(*[spread(x) for x in blocks])]

    for j in range(steps):
        lo = NB * j
        nxt = lo + NB
        inverses = diag_inverses([panel[g, j, lo:nxt, :] for g in range(groups)])
        for g in range(groups):
            li = inverses[g]
            lp = dot3(halves(panel[g, j, lo:, :]), spread(li), NT)
            top = jnp.where(lane - seg_base <= rows, lp[:NB], 0.0)
            if lo % 128:
                panel[g, j, lo // 128 * 128:lo, :] = jnp.zeros((lo % 128, 128), f32)
            panel[g, j, lo:nxt, :] = top
            if nxt < size:
                panel[g, j, nxt:, :] = lp[NB:]
                low = lp[NB:]
                lowh = halves(low)
                for i in range(j + 1, steps, 2):
                    at = NB * (i - j - 1)
                    pair = range(i, min(i + 2, steps))
                    rhs = spread_all([low[NB * (k - j - 1):NB * (k - j)] for k in pair], 0)
                    upd = dot3((lowh[0][at:], lowh[1][at:]), rhs, NT)
                    for n, k in enumerate(pair):
                        panel[g, k, NB * k:, :] -= upd[NB * n:, 128 * n:128 * n + 128]
            if g < n_inv_groups:
                lih = halves(li)
                for c in range(0, j + 1, 2):
                    pair = [k for k in (c, c + 1) if k < j]
                    xs = []
                    if pair:
                        prod = dot3(lih, spread_all([inv[g, k, lo:nxt, :] for k in pair], 1), NN)
                        xs = [prod[:, 128 * n:128 * n + 128] for n in range(len(pair))]
                    if c + len(pair) == j and len(pair) < 2:
                        pair.append(j)
                        xs.append(li)
                    for k, x in zip(pair, xs):
                        inv[g, k, lo:nxt, :] = x
                    if nxt < size:
                        upd = dot3(lowh, spread_all(xs, 1), NN)
                        for n, k in enumerate(pair):
                            piece = upd[:, 128 * n:128 * n + 128]
                            if k == j:
                                inv[g, k, nxt:, :] = -piece
                            else:
                                inv[g, k, nxt:, :] -= piece
                if lo % 128:
                    inv[g, j, lo // 128 * 128:lo, :] = jnp.zeros((lo % 128, 128), f32)

    def unpack(source, into, g, last):
        for j in range(steps):
            begin = NB * j // 128 * 128
            flat = source[g, j, begin:, :].T
            for t in range(4):
                at = 4 * g + t
                if at < last:
                    if begin:
                        into[at, NB * j:NB * j + NB, :begin] = jnp.zeros((NB, begin), f32)
                    into[at, NB * j:NB * j + NB, begin:] = flat[NB * t:NB * t + NB]

    for g in range(n_inv_groups):
        unpack(inv, finv, g, depth + 1)

    stores = []

    def store(src, dst):
        stores.append(pltpu.make_async_copy(src, dst, store_sem.at[len(stores)]))
        stores[-1].start()

    load.wait()
    inverse = jnp.transpose(finv[0]) * math.sqrt(rhs_ref.shape[0] * lax.axis_size("blk"))
    basis_out[...] = dotf(inverse, rhs_in[...], NT)
    store(basis_out, basis_ref)
    for g in range(groups):
        unpack(panel, fact, g, slots)
    for l in range(depth):
        v = halves(pick(finv[l + 1] * math.sqrt(2 * size), hot[l], NN, False))
        second = second_ref[l]
        trans_out[l, pl.ds(pl.multiple_of(second * size, size), size), :] = dot3(halves(fact[l]), v, NN)
        trans_out[l, pl.ds(pl.multiple_of((1 - second) * size, size), size), :] = dot3(
            halves(fact[depth + 1 + l]), v, NN)
        store(trans_out.at[l], trans_ref.at[l])
    for copy in stores:
        copy.wait()


def tri(order, grams, second, rhs):
    depth, size = order.shape
    return pl.pallas_call(
        functools.partial(tri_kernel, 2),
        out_shape=(jax.ShapeDtypeStruct(rhs.shape[::-1], f32), jax.ShapeDtypeStruct((depth, 2 * size, size), f32)),
        in_specs=[pl.BlockSpec(memory_space=pltpu.VMEM), pl.BlockSpec(memory_space=pltpu.VMEM),
                  pl.BlockSpec(memory_space=pltpu.SMEM), pl.BlockSpec(memory_space=pl.ANY)],
        out_specs=[pl.BlockSpec(memory_space=pl.ANY)] * 2,
        scratch_shapes=[
            pltpu.VMEM((depth + 1, size, size), f32),
            pltpu.VMEM((depth, size, size), f32),
            pltpu.VMEM((4, 8, size, 128), f32),
            pltpu.VMEM((2, 8, size, 128), f32),
            pltpu.VMEM((2 * depth + 1, size, size), f32),
            pltpu.VMEM((depth + 1, size, size), f32),
            pltpu.VMEM(rhs.shape, f32),
            pltpu.VMEM(rhs.shape[::-1], f32),
            pltpu.VMEM((depth, 2 * size, size), f32),
            pltpu.SemaphoreType.DMA,
            pltpu.SemaphoreType.DMA((depth + 1,)),
        ],
        compiler_params=pltpu.CompilerParams(vmem_limit_bytes=48 << 20),
    )(order, grams, second, rhs)


MESH = pl.DeviceIdType.MESH


def sum_subtrees(gram, leaf, blk, out_ref, flat, part, run, got, stage, full, sems):
    part_send, part_recv, got_send, got_recv, fwd_send, fwd_recv = sems
    n_blk = lax.axis_size("blk")
    rounds = run.shape[0]
    half = flat.shape[1]
    piece = run.shape[1]

    def mates(r):
        unit = 4 ** r
        digit = (leaf // unit) % 4
        moved = (digit + 1 - 2 * (digit % 2), digit + 2 - 4 * (digit // 2), 3 - digit)
        return [leaf + (m - digit) * unit for m in moved]

    flat[0:half] = gram[0:half, 0:half]
    flat[half:2 * half] = gram[half:, 0:half]
    flat[2 * half:] = gram[half:, half:]
    started = []

    def send(src, dst, s_sem, r_sem, device):
        copy = pltpu.make_async_remote_copy(src_ref=src, dst_ref=dst, send_sem=s_sem, recv_sem=r_sem,
                                            device_id=device, device_id_type=MESH)
        copy.start()
        started.append(copy)
        return copy

    first = []
    for d in range(1, n_blk):
        peer = (blk + d) % n_blk
        first.append(send(flat.at[pl.ds(pl.multiple_of(peer * piece, 8), piece)], part.at[d - 1],
                          part_send.at[d - 1], part_recv.at[d - 1], (leaf, peer)))
    yield
    mine = pl.multiple_of(blk * piece, 8)
    forwards = []

    def forward(slot_at, begin, size):
        for d in range(1, n_blk):
            forwards.append(send(stage.at[pl.ds(begin, size)], full.at[pl.ds(begin, size), pl.ds(mine, piece)],
                                 fwd_send.at[slot_at, d - 1], fwd_recv.at[slot_at, d - 1], (leaf, (blk + d) % n_blk)))

    for copy in first:
        copy.wait_recv()
    run[0] = flat[pl.ds(mine, piece)] + ((part[0] + part[1]) + part[2])
    for r in range(rounds):
        copies = [send(run.at[r], got.at[r, m], got_send.at[r, m], got_recv.at[r, m], (mate, blk))
                  for m, mate in enumerate(mates(r))]
        if r == 0:
            stage[0] = run[0]
            full[0, pl.ds(mine, piece)] = stage[0]
            forward(0, 0, 1)
        else:
            forward(r, 2 * r - 1, 2)
        for copy in copies:
            copy.wait_recv()
        near = got[r, 0]
        far = got[r, 1] + got[r, 2]
        if r + 1 < rounds:
            run[r + 1] = run[r] + near + far
        for k, value in enumerate((near, far)):
            stage[1 + 2 * r + k] = value
            full[1 + 2 * r + k, pl.ds(mine, piece)] = value
    forward(rounds, 2 * rounds - 1, 2)
    for copy in forwards:
        copy.wait_recv()
    for copy in started:
        copy.wait_send()
    out_ref[...] = full[...]


def near_kernel(dims, slot_ref, feat_ref, sketch_ref, omega_ref, sums_ref, rhs_ref,
                hot, back, out_a, out_p, out_s, in_a, in_p, in_s, side, acc, row_aug, gram, off_hi, off_lo,
                flat, part, run, got, stage, full,
                omega_in, sketch_in, load_sem, send_sem, recv_sem, side_send, side_recv, *sum_sems):
    count_x, count_z, count_core = dims
    count = count_x * count_z * count_core
    leaf, blk = lax.axis_index("leaf"), lax.axis_index("blk")
    n_blk = lax.axis_size("blk")
    points = slot_ref.shape[1]
    chunk = points // count
    feats = feat_ref.shape[0]
    groups = 4
    per = count // groups
    rank = omega_ref.shape[0]
    lot = out_a.shape[1]
    low = lot - chunk // 2
    wide = points // groups
    strip = min(128, wide)
    in_strip = strip // chunk
    my_core = leaf % count_core
    my_z = (leaf // count_core) % count_z
    my_x = leaf // (count_core * count_z)
    right, left = (blk + 1) % n_blk, (blk + n_blk - 1) % n_blk

    def target(t):
        a = lax.div(t, count_z)
        core = lax.rem(my_core + lax.div(a, count_x) + t, count_core)
        z = lax.rem(my_z + t * 3, count_z)
        x = lax.rem(my_x + a + t, count_x)
        return (x * count_z + z) * count_core + core

    load_omega = pltpu.make_async_copy(omega_ref, omega_in, load_sem.at[0])
    load_sketch = pltpu.make_async_copy(sketch_ref, sketch_in, load_sem.at[1])
    load_omega.start()
    load_sketch.start()
    barrier = pltpu.get_barrier_semaphore()

    @pl.loop(1, count)
    def _(t):
        pl.semaphore_signal(barrier, inc=1, device_id=(target(t), blk), device_id_type=MESH)

    for peer in [(blk + d) % n_blk for d in range(1, n_blk)]:
        pl.semaphore_signal(barrier, inc=1, device_id=(leaf, peer), device_id_type=MESH)

    own = slot_ref[...]
    bits = lambda n: n.bit_length() - 1
    goal = own >> bits(points * n_blk)
    dc = ((goal & (count_core - 1)) - my_core) & (count_core - 1)
    dz = (((goal >> bits(count_core)) & (count_z - 1)) - my_z) & (count_z - 1)
    dx = ((goal >> bits(count_core * count_z)) - my_x) & (count_x - 1)
    turn = (dz * 3) & (count_z - 1)
    a = ((dx - turn) & (count_x - 1)) + count_x * ((dc - turn) & (count_core - 1))
    shift = chunk * (turn + count_z * a - goal)
    own_row = own.astype(f32)
    own_col = jnp.transpose(jnp.broadcast_to(own_row, (128, points)))
    at = lax.broadcasted_iota(jnp.int32, (points, 128), 0)
    for c in range(points // 128):
        lanes = slice(128 * c, 128 * c + 128)
        place = jnp.sum(jnp.where(own_col < own_row[:, lanes], 1.0, 0.0), axis=0, keepdims=True).astype(jnp.int32)
        hot[:, lanes] = jnp.where(at == place + shift[:, lanes], 1.0, 0.0).astype(bf16)

    fh, fl = halves(jnp.concatenate([feat_ref[...]] * 2, axis=0))
    ph, pl_low = halves(jnp.broadcast_to((own & (points - 1)).astype(f32), (16, points)))
    first = lax.broadcasted_iota(jnp.int32, (in_strip, chunk // 2, 2 * feats), 2) < feats
    load_omega.wait()
    oh, ol = halves(omega_in[...])

    pairs = ((out_a, in_a), (out_s, in_s), (out_p, in_p))

    def moves(t, which):
        src, dst = pairs[which]
        return pltpu.make_async_remote_copy(
            src_ref=src.at[pl.ds(lax.div(t, in_strip) if which == 2 else t, 1)], dst_ref=dst.at[pl.ds(t, 1)],
            send_sem=send_sem.at[which], recv_sem=recv_sem.at[which, lax.div(t, per)],
            device_id=(target(t), blk), device_id_type=MESH)

    def whole(begin, end, which, g):
        into = pairs[which][1].at[pl.ds(begin, end - begin)]
        return pltpu.make_async_remote_copy(
            src_ref=into, dst_ref=into, send_sem=send_sem.at[which], recv_sem=recv_sem.at[which, g],
            device_id=(target(1), blk), device_id_type=MESH)

    def arrived(g, which):
        return whole(max(1, g * per), (g + 1) * per, which, g)

    for r in range(points // strip):
        h = hot[strip * r:strip * r + strip, :]
        lots = slice(in_strip * r, in_strip * r + in_strip)
        value = mm(h, oh, NT) + mm(h, ol, NT)
        for n in range(rank // 128):
            out_a[lots, chunk * n:chunk * n + chunk, :] = jnp.reshape(
                value[:, 128 * n:128 * n + 128], (in_strip, chunk, 128))
        value = jnp.reshape(mm(h, fh, NT) + mm(h, fl, NT), (in_strip, chunk, 2 * feats))
        out_a[lots, low:, 0:2 * feats] = jnp.where(first, value[:, :chunk // 2], value[:, chunk // 2:])
        out_p[r] = (mm(ph, h, NT) + mm(pl_low, h, NT))[0:1]
        if r == 0:
            pl.semaphore_wait(barrier, count - 1 + n_blk - 1)

        @pl.loop(max(1, in_strip * r), in_strip * r + in_strip)
        def _(t):
            moves(t, 0).start()

    load_sketch.wait()
    sh, sl = halves(sketch_in[...])
    for r in range(points // strip):
        h = hot[strip * r:strip * r + strip, :]
        out_s[in_strip * r:in_strip * r + in_strip] = jnp.reshape(
            mm(h, sh, NT) + mm(h, sl, NT), (in_strip, chunk, rank))

        @pl.loop(max(1, in_strip * r), in_strip * r + in_strip)
        def _(t):
            moves(t, 1).start()

    @pl.loop(1, count)
    def _(t):
        moves(t, 2).start()

    in_a[0] = out_a[0]
    in_s[0] = out_s[0]
    in_p[0] = out_p[0]

    def own_side(g, way):
        peer, slot_at = ((right, 0), (left, 1))[way]
        rows = pl.ds(g * per, per)
        return pltpu.make_async_remote_copy(
            src_ref=in_a.at[rows], dst_ref=side.at[slot_at, rows], send_sem=side_send.at[way, g],
            recv_sem=side_recv.at[slot_at, g], device_id=(leaf, peer), device_id_type=MESH)

    def relay(g, way):
        peer = (right, left)[way]
        rows = pl.ds((2 * g + way) * (per // 2), per // 2)
        return pltpu.make_async_remote_copy(
            src_ref=side.at[way, rows], dst_ref=side.at[2, rows], send_sem=side_send.at[2 + way, g],
            recv_sem=side_recv.at[2 + way, g], device_id=(leaf, peer), device_id_type=MESH)

    scale = -2.0 / feats * math.log2(math.e)

    def feats_of(lots):
        cut = lots[:, low:, 0:2 * feats]
        return jnp.reshape(jnp.concatenate([cut[:, :, :feats], cut[:, :, feats:]], axis=1), (wide, feats))

    def omegas_of(lots):
        return jnp.concatenate([jnp.reshape(lots[:, chunk * n:chunk * n + chunk], (wide, 128))
                                for n in range(rank // 128)], axis=1)

    one = jnp.ones((wide, 1), bf16)
    fill = jnp.zeros((wide, 256 - 3 * feats - 6), bf16)

    def arrive(g):
        arrived(g, 0).wait_recv()
        for way in range(2):
            own_side(g, way).start()
        x = feats_of(in_a[g * per:g * per + per])
        norm = thirds(jnp.sum(x * x, axis=1, keepdims=True) * scale)
        xh, xl = halves(x * (-2.0 * scale))
        row_aug[g * wide:g * wide + wide, :] = jnp.concatenate([xh, xh, xl, *norm, one, one, one, fill], axis=1)

    def hand_on(g):
        for way in range(2):
            own_side(g, way).wait_recv()
            relay(g, way).start()

    def absorb(block):
        x = feats_of(block)
        xh, xl = halves(x)
        norm = thirds(jnp.sum(x * x, axis=1, keepdims=True) * scale)
        col_aug = jnp.concatenate([xh, xl, xh, one, one, one, *norm, fill], axis=1)
        om = halves(omegas_of(block))
        for a in range(groups):
            rows = slice(a * wide, a * wide + wide)
            value = jnp.exp2(mm(row_aug[rows, :], col_aug, NT))
            acc[rows, :] += dot3(halves(value), om, NN)

    arrive(0)
    for g in range(1, groups):
        arrive(g)
        hand_on(g - 1)
    acc[...] = jnp.zeros_like(acc)

    @pl.loop(0, groups)
    def _(g):
        absorb(in_a[pl.ds(g * per, per)])

    hand_on(groups - 1)

    @pl.loop(0, 2 * groups)
    def _(i):
        absorb(side[lax.div(i, groups), pl.ds(lax.rem(i, groups) * per, per)])

    @pl.loop(0, groups)
    def _(g):
        for way in range(2):
            relay(g, way).wait_recv()
        absorb(side[2, pl.ds(g * per, per)])

    for g in range(groups):
        arrived(g, 1).wait_recv()
        rows = slice(g * wide, g * wide + wide)
        off = halves(jnp.reshape(in_s[g * per:g * per + per], (wide, rank)) - acc[rows, :])
        off_hi[rows, :], off_lo[rows, :] = off
        term = dot3(off, off, TN)
        if g == 0:
            gram[...] = term
        else:
            gram[...] += term

    steps = sum_subtrees(gram, leaf, blk, sums_ref, flat, part, run, got, stage, full, sum_sems)
    next(steps)
    for g in range(groups):
        arrived(g, 2).wait_recv()
    sub = lax.broadcasted_iota(jnp.int32, (in_strip, 1, strip), 0)
    lane = lax.broadcasted_iota(jnp.int32, (in_strip, 1, strip), 2)
    down = lax.broadcasted_iota(jnp.int32, (points, strip), 0)
    for u in range(points // strip):
        mine = jnp.where(lane // chunk == sub, in_p[u * in_strip:(u + 1) * in_strip], 0.0)
        row = jnp.sum(mine, axis=0).astype(jnp.int32)
        back[:, u * strip:(u + 1) * strip] = jnp.where(down == row, 1.0, 0.0).astype(bf16)
    for r in range(groups):
        rows = slice(r * wide, r * wide + wide)
        rhs_ref[rows, :] = mm(back[rows, :], off_hi[...], NN) + mm(back[rows, :], off_lo[...], NN)
    for _ in steps:
        pass

    for which in range(3):
        whole(1, count, which, 0).wait_send()

    @pl.loop(0, groups)
    def _(g):
        for way in range(2):
            own_side(g, way).wait_send()
            relay(g, way).wait_send()


def near_field(slot, features, sketch, omega, depth):
    feats, points = features.shape
    rank = sketch.shape[0]
    count = lax.axis_size("leaf")
    n_blk = lax.axis_size("blk")
    core = 2
    z = min(8, count // core)
    dims = (count // (core * z), z, core)
    half = rank // 2
    lines = 3 * half
    piece = lines // n_blk
    rounds = depth // 2
    chunk = points // count
    lot = rank // 128 * chunk + chunk // 2
    strip = min(128, points // 4)
    vm = lambda *shape: pltpu.VMEM(shape, f32)
    vb = lambda *shape: pltpu.VMEM(shape, bf16)
    dma = lambda *shape: pltpu.SemaphoreType.DMA(shape)
    return pl.pallas_call(
        functools.partial(near_kernel, dims),
        out_shape=(jax.ShapeDtypeStruct((depth + 1, lines, half), f32), jax.ShapeDtypeStruct((points, rank), f32)),
        in_specs=[pl.BlockSpec(memory_space=pltpu.VMEM)] * 2 + [pl.BlockSpec(memory_space=pl.ANY)] * 2,
        out_specs=[pl.BlockSpec(memory_space=pltpu.VMEM)] * 2,
        scratch_shapes=[
            vb(points, points), vb(points, points),
            vm(count, lot, 128), vm(points // strip, 1, strip), vm(count, chunk, rank),
            vm(count, lot, 128), vm(count, 1, strip), vm(count, chunk, rank),
            vm(3, count, lot, 128), vm(points, rank), vb(points, 256), vm(rank, rank),
            vb(points, rank), vb(points, rank),
            vm(lines, half), vm(n_blk - 1, piece, half), vm(rounds, piece, half), vm(rounds, 3, piece, half),
            vm(depth + 1, piece, half), vm(depth + 1, lines, half),
            vm(rank, points), vm(rank, points), dma(2), dma(3), dma(3, 4), dma(4, 4), dma(4, 4),
            dma(n_blk - 1), dma(n_blk - 1), dma(rounds, 3), dma(rounds, 3),
            dma(rounds + 1, n_blk - 1), dma(rounds + 1, n_blk - 1),
        ],
        compiler_params=pltpu.CompilerParams(collective_id=0, has_side_effects=True, vmem_limit_bytes=63 << 20),
    )(slot[None], features, sketch, omega)


def per_device(features, sketch, omega, slot, column_order):
    depth = column_order.shape[0]
    sums, turned = near_field(slot, features, sketch, omega, depth)
    second = lax.axis_index("leaf") >> jnp.arange(depth, dtype=jnp.int32) & 1
    leaf_basis, transfers = tri(column_order, sums, second, turned)
    return (leaf_basis, transfers[None])


def solution(mesh):
    placed = (
        P(None, ("leaf", "blk")),
        P(None, ("leaf", "blk")),
        P(None, ("leaf", "blk")),
        P(("leaf", "blk")),
        P(),
    )
    return jax.shard_map(
        per_device,
        mesh=mesh,
        in_specs=placed,
        out_specs=(P(None, ("leaf", "blk")), P("leaf", None, None, None)),
        check_vma=False,
    )
```

```python
import functools
import math

import jax
import jax.numpy as jnp
from jax import lax
from jax.experimental import pallas as pl
from jax.experimental.pallas import tpu as pltpu
from jax.sharding import PartitionSpec as P

NN = (((1,), (0,)), ((), ()))
NT = (((1,), (1,)), ((), ()))
TN = (((0,), (0,)), ((), ()))
f32, bf16 = jnp.float32, jnp.bfloat16


def mm(a, b, dims):
    return lax.dot_general(a, b, dims, preferred_element_type=f32)


def halves(x):
    hi = x.astype(bf16)
    return hi, (x - hi.astype(f32)).astype(bf16)


def thirds(x):
    hi = x.astype(bf16)
    rest = x - hi.astype(f32)
    mid = rest.astype(bf16)
    return hi, mid, (rest - mid.astype(f32)).astype(bf16)


def dot3(a, b, dims):
    return mm(a[0], b[0], dims) + (mm(a[0], b[1], dims) + mm(a[1], b[0], dims))


def dotf(a, b, dims):
    return dot3(halves(a), halves(b), dims)


def pick(x, hot, dims, left):
    hi, lo = halves(x)
    if left:
        return mm(hi, hot, dims) + mm(lo, hot, dims)
    return mm(hot, hi, dims) + mm(hot, lo, dims)


NB = 32
TILE = 8


def spread_row(x, i):
    return jnp.broadcast_to(x[i:i + 1, :], x.shape)


def diag_inverses(blocks):
    tiles = NB // TILE
    width = 128 * len(blocks)
    a = [jnp.concatenate([x[TILE * q:TILE * q + TILE] for x in blocks], axis=1) for q in range(tiles)]
    lane = lax.broadcasted_iota(jnp.int32, (TILE, width), 1) % NB
    row = lax.broadcasted_iota(jnp.int32, (TILE, width), 0)
    base = lax.broadcasted_iota(jnp.int32, (TILE, 128), 1) // NB * NB
    b = [jnp.where(lane == row + TILE * q, 1.0, 0.0).astype(f32) for q in range(tiles)]

    def column(x, k):
        return jnp.concatenate(
            [jnp.take_along_axis(x[:, 128 * g:128 * g + 128], base + k, axis=1, mode="promise_in_bounds")
             for g in range(len(blocks))], axis=1)

    done = []
    for p in range(tiles):
        below = range(p, tiles)
        cols = [{q: column(a[q], TILE * p + i) for q in below} for i in range(TILE)]
        mult = []
        scale = jnp.zeros((TILE, width), f32)
        for i in range(TILE):
            root = lax.rsqrt(spread_row(cols[i][p], i))
            scale = jnp.where(row == i, root, scale)
            m = {q: cols[i][q] * (root * root) for q in below}
            m[p] = jnp.where(row > i, m[p], 0.0)
            mult.append(m)
            for t in range(i + 1, TILE):
                head = spread_row(cols[t][p], i)
                for q in below:
                    cols[t][q] = cols[t][q] - m[q] * head
            if i + 1 < TILE:
                a[p] = a[p] - m[p] * spread_row(a[p], i)
                b[p] = b[p] - m[p] * spread_row(b[p], i)
        for i in range(TILE):
            ra, rb = spread_row(a[p], i), spread_row(b[p], i)
            for q in range(p + 1, tiles):
                a[q] = a[q] - mult[i][q] * ra
                b[q] = b[q] - mult[i][q] * rb
        done.append(b[p] * scale)
    whole = jnp.concatenate(done, axis=0)
    return [whole[:, 128 * g:128 * g + 128] for g in range(len(blocks))]


def tri_kernel(n_inv_groups, order_ref, gram_ref, second_ref, rhs_ref, basis_ref, trans_ref,
               own, sib, panel, inv, fact, finv, rhs_in, basis_out, trans_out, order_in, gram_in, load_sem, store_sem):
    groups = 4
    size = order_ref.shape[1]
    half = size // 2
    steps = size // NB
    depth = order_ref.shape[0]
    load_order = pltpu.make_async_copy(order_ref, order_in, load_sem.at[0])
    load_grams = pltpu.make_async_copy(gram_ref, gram_in, load_sem.at[2])
    load = pltpu.make_async_copy(rhs_ref, rhs_in, load_sem.at[1])
    for copy in (load_order, load_grams, load):
        copy.start()
    load_order.wait()
    load_grams.wait()
    slots = 2 * depth + 1
    isub = lax.broadcasted_iota(jnp.int32, (size, size), 0)
    hot = [jnp.where(isub == order_in[l:l + 1, :], 1.0, 0.0).astype(bf16) for l in range(depth)]
    total = [hot[0]]
    for l in range(1, depth):
        total.append(mm(total[-1], hot[l], NN).astype(bf16))

    def reorder(g, q):
        return pick(pick(g, q, NN, True), q, TN, False)

    def unfold(at):
        low = gram_in[at, half:2 * half, :]
        top = jnp.concatenate([gram_in[at, 0:half, :], jnp.transpose(low)], axis=1)
        return jnp.concatenate([top, jnp.concatenate([low, gram_in[at, 2 * half:, :]], axis=1)], axis=0)

    running = unfold(0)
    own[0] = running
    for l in range(depth):
        g = unfold(l + 1)
        sib[l] = g if l == 0 else reorder(g, total[l - 1])
        running = running + g
        own[l + 1] = reorder(running, total[l])

    def dense(s):
        if s <= depth:
            return own, s
        return sib, min(s - depth - 1, depth - 1)

    for j in range(steps):
        for g in range(groups):
            lo = NB * j
            pieces = []
            for t in range(4):
                ref, at = dense(min(4 * g + t, slots - 1))
                pieces.append(ref[at, lo:lo + NB, lo // 128 * 128:])
            panel[g, j, lo // 128 * 128:, :] = jnp.concatenate(pieces, axis=0).T

    lane = lax.broadcasted_iota(jnp.int32, (NB, 128), 1)
    rows = lax.broadcasted_iota(jnp.int32, (NB, 128), 0)
    seg_base = (lane // NB) * NB
    r128 = lax.broadcasted_iota(jnp.int32, (128, 128), 0) // NB
    l128 = lax.broadcasted_iota(jnp.int32, (128, 128), 1) // NB
    same = r128 == l128

    same = jnp.where(same, 1.0, 0.0).astype(bf16)

    def spread(x):
        return [jnp.concatenate([part] * 4, axis=0) * same for part in halves(x)]

    def spread_all(blocks, axis):
        return [jnp.concatenate(parts, axis=axis) for parts in zip(*[spread(x) for x in blocks])]

    for j in range(steps):
        lo = NB * j
        nxt = lo + NB
        inverses = diag_inverses([panel[g, j, lo:nxt, :] for g in range(groups)])
        for g in range(groups):
            li = inverses[g]
            lp = dot3(halves(panel[g, j, lo:, :]), spread(li), NT)
            top = jnp.where(lane - seg_base <= rows, lp[:NB], 0.0)
            if lo % 128:
                panel[g, j, lo // 128 * 128:lo, :] = jnp.zeros((lo % 128, 128), f32)
            panel[g, j, lo:nxt, :] = top
            if nxt < size:
                panel[g, j, nxt:, :] = lp[NB:]
                low = lp[NB:]
                lowh = halves(low)
                for i in range(j + 1, steps, 2):
                    at = NB * (i - j - 1)
                    pair = range(i, min(i + 2, steps))
                    rhs = spread_all([low[NB * (k - j - 1):NB * (k - j)] for k in pair], 0)
                    upd = dot3((lowh[0][at:], lowh[1][at:]), rhs, NT)
                    for n, k in enumerate(pair):
                        panel[g, k, NB * k:, :] -= upd[NB * n:, 128 * n:128 * n + 128]
            if g < n_inv_groups:
                lih = halves(li)
                for c in range(0, j + 1, 2):
                    pair = [k for k in (c, c + 1) if k < j]
                    xs = []
                    if pair:
                        prod = dot3(lih, spread_all([inv[g, k, lo:nxt, :] for k in pair], 1), NN)
                        xs = [prod[:, 128 * n:128 * n + 128] for n in range(len(pair))]
                    if c + len(pair) == j and len(pair) < 2:
                        pair.append(j)
                        xs.append(li)
                    for k, x in zip(pair, xs):
                        inv[g, k, lo:nxt, :] = x
                    if nxt < size:
                        upd = dot3(lowh, spread_all(xs, 1), NN)
                        for n, k in enumerate(pair):
                            piece = upd[:, 128 * n:128 * n + 128]
                            if k == j:
                                inv[g, k, nxt:, :] = -piece
                            else:
                                inv[g, k, nxt:, :] -= piece
                if lo % 128:
                    inv[g, j, lo // 128 * 128:lo, :] = jnp.zeros((lo % 128, 128), f32)

    def unpack(source, into, g, last):
        for j in range(steps):
            begin = NB * j // 128 * 128
            flat = source[g, j, begin:, :].T
            for t in range(4):
                at = 4 * g + t
                if at < last:
                    if begin:
                        into[at, NB * j:NB * j + NB, :begin] = jnp.zeros((NB, begin), f32)
                    into[at, NB * j:NB * j + NB, begin:] = flat[NB * t:NB * t + NB]

    for g in range(n_inv_groups):
        unpack(inv, finv, g, depth + 1)

    stores = []

    def store(src, dst):
        stores.append(pltpu.make_async_copy(src, dst, store_sem.at[len(stores)]))
        stores[-1].start()

    load.wait()
    inverse = jnp.transpose(finv[0]) * math.sqrt(rhs_ref.shape[0] * lax.axis_size("blk"))
    basis_out[...] = dotf(inverse, rhs_in[...], NT)
    store(basis_out, basis_ref)
    for g in range(groups):
        unpack(panel, fact, g, slots)
    for l in range(depth):
        v = halves(pick(finv[l + 1] * math.sqrt(2 * size), hot[l], NN, False))
        second = second_ref[l]
        trans_out[l, pl.ds(pl.multiple_of(second * size, size), size), :] = dot3(halves(fact[l]), v, NN)
        trans_out[l, pl.ds(pl.multiple_of((1 - second) * size, size), size), :] = dot3(
            halves(fact[depth + 1 + l]), v, NN)
        store(trans_out.at[l], trans_ref.at[l])
    for copy in stores:
        copy.wait()


def tri(order, grams, second, rhs):
    depth, size = order.shape
    return pl.pallas_call(
        functools.partial(tri_kernel, 2),
        out_shape=(jax.ShapeDtypeStruct(rhs.shape[::-1], f32), jax.ShapeDtypeStruct((depth, 2 * size, size), f32)),
        in_specs=[pl.BlockSpec(memory_space=pltpu.HBM), pl.BlockSpec(memory_space=pltpu.HBM),
                  pl.BlockSpec(memory_space=pltpu.SMEM), pl.BlockSpec(memory_space=pltpu.HBM)],
        out_specs=[pl.BlockSpec(memory_space=pl.ANY)] * 2,
        scratch_shapes=[
            pltpu.VMEM((depth + 1, size, size), f32),
            pltpu.VMEM((depth, size, size), f32),
            pltpu.VMEM((4, 8, size, 128), f32),
            pltpu.VMEM((2, 8, size, 128), f32),
            pltpu.VMEM((2 * depth + 1, size, size), f32),
            pltpu.VMEM((depth + 1, size, size), f32),
            pltpu.VMEM(rhs.shape, f32),
            pltpu.VMEM(rhs.shape[::-1], f32),
            pltpu.VMEM((depth, 2 * size, size), f32),
            pltpu.VMEM(order.shape, jnp.int32),
            pltpu.VMEM(grams.shape, f32),
            pltpu.SemaphoreType.DMA((3,)),
            pltpu.SemaphoreType.DMA((depth + 1,)),
        ],
        compiler_params=pltpu.CompilerParams(vmem_limit_bytes=48 << 20),
    )(order, grams, second, rhs)


MESH = pl.DeviceIdType.MESH


def sum_subtrees(gram, leaf, blk, out_ref, flat, part, run, got, stage, full, sems):
    part_send, part_recv, got_send, got_recv, fwd_send, fwd_recv = sems
    n_blk = lax.axis_size("blk")
    rounds = run.shape[0]
    half = flat.shape[1]
    piece = run.shape[1]

    def mates(r):
        unit = 4 ** r
        digit = (leaf // unit) % 4
        moved = (digit + 1 - 2 * (digit % 2), digit + 2 - 4 * (digit // 2), 3 - digit)
        return [leaf + (m - digit) * unit for m in moved]

    flat[0:half] = gram[0:half, 0:half]
    flat[half:2 * half] = gram[half:, 0:half]
    flat[2 * half:] = gram[half:, half:]
    started = []

    def send(src, dst, s_sem, r_sem, device):
        copy = pltpu.make_async_remote_copy(src_ref=src, dst_ref=dst, send_sem=s_sem, recv_sem=r_sem,
                                            device_id=device, device_id_type=MESH)
        copy.start()
        started.append(copy)
        return copy

    first = []
    for d in range(1, n_blk):
        peer = (blk + d) % n_blk
        first.append(send(flat.at[pl.ds(pl.multiple_of(peer * piece, 8), piece)], part.at[d - 1],
                          part_send.at[d - 1], part_recv.at[d - 1], (leaf, peer)))
    yield
    mine = pl.multiple_of(blk * piece, 8)
    forwards = []

    def forward(slot_at, begin, size):
        for d in range(1, n_blk):
            forwards.append(send(stage.at[pl.ds(begin, size)], full.at[pl.ds(begin, size), pl.ds(mine, piece)],
                                 fwd_send.at[slot_at, d - 1], fwd_recv.at[slot_at, d - 1], (leaf, (blk + d) % n_blk)))

    for copy in first:
        copy.wait_recv()
    run[0] = flat[pl.ds(mine, piece)] + ((part[0] + part[1]) + part[2])
    for r in range(rounds):
        copies = [send(run.at[r], got.at[r, m], got_send.at[r, m], got_recv.at[r, m], (mate, blk))
                  for m, mate in enumerate(mates(r))]
        if r == 0:
            stage[0] = run[0]
            full[0, pl.ds(mine, piece)] = stage[0]
            forward(0, 0, 1)
        else:
            forward(r, 2 * r - 1, 2)
        for copy in copies:
            copy.wait_recv()
        near = got[r, 0]
        far = got[r, 1] + got[r, 2]
        if r + 1 < rounds:
            run[r + 1] = run[r] + near + far
        for k, value in enumerate((near, far)):
            stage[1 + 2 * r + k] = value
            full[1 + 2 * r + k, pl.ds(mine, piece)] = value
    forward(rounds, 2 * rounds - 1, 2)
    for copy in forwards:
        copy.wait_recv()
    for copy in started:
        copy.wait_send()
    out_ref[...] = full[...]


def near_kernel(dims, slot_ref, feat_ref, sketch_ref, omega_ref, sums_ref, rhs_ref,
                hot, back, out_a, out_p, out_s, in_a, in_p, in_s, side, acc, row_aug, gram, off_hi, off_lo,
                flat, part, run, got, stage, full,
                omega_in, sketch_in, load_sem, send_sem, recv_sem, side_send, side_recv, *sum_sems):
    count_x, count_z, count_core = dims
    count = count_x * count_z * count_core
    leaf, blk = lax.axis_index("leaf"), lax.axis_index("blk")
    n_blk = lax.axis_size("blk")
    points = slot_ref.shape[1]
    chunk = points // count
    feats = feat_ref.shape[0]
    groups = 4
    per = count // groups
    rank = omega_ref.shape[0]
    lot = out_a.shape[1]
    low = lot - chunk // 2
    wide = points // groups
    strip = min(128, wide)
    in_strip = strip // chunk
    my_core = leaf % count_core
    my_z = (leaf // count_core) % count_z
    my_x = leaf // (count_core * count_z)
    right, left = (blk + 1) % n_blk, (blk + n_blk - 1) % n_blk

    def target(t):
        a = lax.div(t, count_z)
        core = lax.rem(my_core + lax.div(a, count_x) + t, count_core)
        z = lax.rem(my_z + t * 3, count_z)
        x = lax.rem(my_x + a + t, count_x)
        return (x * count_z + z) * count_core + core

    load_omega = pltpu.make_async_copy(omega_ref, omega_in, load_sem.at[0])
    load_sketch = pltpu.make_async_copy(sketch_ref, sketch_in, load_sem.at[1])
    load_omega.start()
    load_sketch.start()
    barrier = pltpu.get_barrier_semaphore()

    @pl.loop(1, count)
    def _(t):
        pl.semaphore_signal(barrier, inc=1, device_id=(target(t), blk), device_id_type=MESH)

    for peer in [(blk + d) % n_blk for d in range(1, n_blk)]:
        pl.semaphore_signal(barrier, inc=1, device_id=(leaf, peer), device_id_type=MESH)

    own = slot_ref[...]
    bits = lambda n: n.bit_length() - 1
    goal = own >> bits(points * n_blk)
    dc = ((goal & (count_core - 1)) - my_core) & (count_core - 1)
    dz = (((goal >> bits(count_core)) & (count_z - 1)) - my_z) & (count_z - 1)
    dx = ((goal >> bits(count_core * count_z)) - my_x) & (count_x - 1)
    turn = (dz * 3) & (count_z - 1)
    a = ((dx - turn) & (count_x - 1)) + count_x * ((dc - turn) & (count_core - 1))
    shift = chunk * (turn + count_z * a - goal)
    own_row = own.astype(f32)
    own_col = jnp.transpose(jnp.broadcast_to(own_row, (128, points)))
    at = lax.broadcasted_iota(jnp.int32, (points, 128), 0)
    for c in range(points // 128):
        lanes = slice(128 * c, 128 * c + 128)
        place = jnp.sum(jnp.where(own_col < own_row[:, lanes], 1.0, 0.0), axis=0, keepdims=True).astype(jnp.int32)
        hot[:, lanes] = jnp.where(at == place + shift[:, lanes], 1.0, 0.0).astype(bf16)

    fh, fl = halves(jnp.concatenate([feat_ref[...]] * 2, axis=0))
    ph, pl_low = halves(jnp.broadcast_to((own & (points - 1)).astype(f32), (16, points)))
    first = lax.broadcasted_iota(jnp.int32, (in_strip, chunk // 2, 2 * feats), 2) < feats
    load_omega.wait()
    oh, ol = halves(omega_in[...])

    pairs = ((out_a, in_a), (out_s, in_s), (out_p, in_p))

    def moves(t, which):
        src, dst = pairs[which]
        return pltpu.make_async_remote_copy(
            src_ref=src.at[pl.ds(lax.div(t, in_strip) if which == 2 else t, 1)], dst_ref=dst.at[pl.ds(t, 1)],
            send_sem=send_sem.at[which], recv_sem=recv_sem.at[which, lax.div(t, per)],
            device_id=(target(t), blk), device_id_type=MESH)

    def whole(begin, end, which, g):
        into = pairs[which][1].at[pl.ds(begin, end - begin)]
        return pltpu.make_async_remote_copy(
            src_ref=into, dst_ref=into, send_sem=send_sem.at[which], recv_sem=recv_sem.at[which, g],
            device_id=(target(1), blk), device_id_type=MESH)

    def arrived(g, which):
        return whole(max(1, g * per), (g + 1) * per, which, g)

    for r in range(points // strip):
        h = hot[strip * r:strip * r + strip, :]
        lots = slice(in_strip * r, in_strip * r + in_strip)
        value = mm(h, oh, NT) + mm(h, ol, NT)
        for n in range(rank // 128):
            out_a[lots, chunk * n:chunk * n + chunk, :] = jnp.reshape(
                value[:, 128 * n:128 * n + 128], (in_strip, chunk, 128))
        value = jnp.reshape(mm(h, fh, NT) + mm(h, fl, NT), (in_strip, chunk, 2 * feats))
        out_a[lots, low:, 0:2 * feats] = jnp.where(first, value[:, :chunk // 2], value[:, chunk // 2:])
        out_p[r] = (mm(ph, h, NT) + mm(pl_low, h, NT))[0:1]
        if r == 0:
            pl.semaphore_wait(barrier, count - 1 + n_blk - 1)

        @pl.loop(max(1, in_strip * r), in_strip * r + in_strip)
        def _(t):
            moves(t, 0).start()

    load_sketch.wait()
    sh, sl = halves(sketch_in[...])
    for r in range(points // strip):
        h = hot[strip * r:strip * r + strip, :]
        out_s[in_strip * r:in_strip * r + in_strip] = jnp.reshape(
            mm(h, sh, NT) + mm(h, sl, NT), (in_strip, chunk, rank))

        @pl.loop(max(1, in_strip * r), in_strip * r + in_strip)
        def _(t):
            moves(t, 1).start()

    @pl.loop(1, count)
    def _(t):
        moves(t, 2).start()

    in_a[0] = out_a[0]
    in_s[0] = out_s[0]
    in_p[0] = out_p[0]

    def own_side(g, way):
        peer, slot_at = ((right, 0), (left, 1))[way]
        rows = pl.ds(g * per, per)
        return pltpu.make_async_remote_copy(
            src_ref=in_a.at[rows], dst_ref=side.at[slot_at, rows], send_sem=side_send.at[way, g],
            recv_sem=side_recv.at[slot_at, g], device_id=(leaf, peer), device_id_type=MESH)

    def relay(g, way):
        peer = (right, left)[way]
        rows = pl.ds((2 * g + way) * (per // 2), per // 2)
        return pltpu.make_async_remote_copy(
            src_ref=side.at[way, rows], dst_ref=side.at[2, rows], send_sem=side_send.at[2 + way, g],
            recv_sem=side_recv.at[2 + way, g], device_id=(leaf, peer), device_id_type=MESH)

    scale = -2.0 / feats * math.log2(math.e)

    def feats_of(lots):
        cut = lots[:, low:, 0:2 * feats]
        return jnp.reshape(jnp.concatenate([cut[:, :, :feats], cut[:, :, feats:]], axis=1), (wide, feats))

    def omegas_of(lots):
        return jnp.concatenate([jnp.reshape(lots[:, chunk * n:chunk * n + chunk], (wide, 128))
                                for n in range(rank // 128)], axis=1)

    one = jnp.ones((wide, 1), bf16)
    fill = jnp.zeros((wide, 256 - 3 * feats - 6), bf16)

    def arrive(g):
        arrived(g, 0).wait_recv()
        for way in range(2):
            own_side(g, way).start()
        x = feats_of(in_a[g * per:g * per + per])
        norm = thirds(jnp.sum(x * x, axis=1, keepdims=True) * scale)
        xh, xl = halves(x * (-2.0 * scale))
        row_aug[g * wide:g * wide + wide, :] = jnp.concatenate([xh, xh, xl, *norm, one, one, one, fill], axis=1)

    def hand_on(g):
        for way in range(2):
            own_side(g, way).wait_recv()
            relay(g, way).start()

    def absorb(block):
        x = feats_of(block)
        xh, xl = halves(x)
        norm = thirds(jnp.sum(x * x, axis=1, keepdims=True) * scale)
        col_aug = jnp.concatenate([xh, xl, xh, one, one, one, *norm, fill], axis=1)
        om = halves(omegas_of(block))
        for a in range(groups):
            rows = slice(a * wide, a * wide + wide)
            value = jnp.exp2(mm(row_aug[rows, :], col_aug, NT))
            acc[rows, :] += dot3(halves(value), om, NN)

    arrive(0)
    for g in range(1, groups):
        arrive(g)
        hand_on(g - 1)
    acc[...] = jnp.zeros_like(acc)

    @pl.loop(0, groups)
    def _(g):
        absorb(in_a[pl.ds(g * per, per)])

    hand_on(groups - 1)

    @pl.loop(0, 2 * groups)
    def _(i):
        absorb(side[lax.div(i, groups), pl.ds(lax.rem(i, groups) * per, per)])

    @pl.loop(0, groups)
    def _(g):
        for way in range(2):
            relay(g, way).wait_recv()
        absorb(side[2, pl.ds(g * per, per)])

    for g in range(groups):
        arrived(g, 1).wait_recv()
        rows = slice(g * wide, g * wide + wide)
        off = halves(jnp.reshape(in_s[g * per:g * per + per], (wide, rank)) - acc[rows, :])
        off_hi[rows, :], off_lo[rows, :] = off
        term = dot3(off, off, TN)
        if g == 0:
            gram[...] = term
        else:
            gram[...] += term

    steps = sum_subtrees(gram, leaf, blk, sums_ref, flat, part, run, got, stage, full, sum_sems)
    next(steps)
    for g in range(groups):
        arrived(g, 2).wait_recv()
    sub = lax.broadcasted_iota(jnp.int32, (in_strip, 1, strip), 0)
    lane = lax.broadcasted_iota(jnp.int32, (in_strip, 1, strip), 2)
    down = lax.broadcasted_iota(jnp.int32, (points, strip), 0)
    for u in range(points // strip):
        mine = jnp.where(lane // chunk == sub, in_p[u * in_strip:(u + 1) * in_strip], 0.0)
        row = jnp.sum(mine, axis=0).astype(jnp.int32)
        back[:, u * strip:(u + 1) * strip] = jnp.where(down == row, 1.0, 0.0).astype(bf16)
    for r in range(groups):
        rows = slice(r * wide, r * wide + wide)
        rhs_ref[rows, :] = mm(back[rows, :], off_hi[...], NN) + mm(back[rows, :], off_lo[...], NN)
    for _ in steps:
        pass

    for which in range(3):
        whole(1, count, which, 0).wait_send()

    @pl.loop(0, groups)
    def _(g):
        for way in range(2):
            own_side(g, way).wait_send()
            relay(g, way).wait_send()


def near_field(slot, features, sketch, omega, depth):
    feats, points = features.shape
    rank = sketch.shape[0]
    count = lax.axis_size("leaf")
    n_blk = lax.axis_size("blk")
    core = 2
    z = min(8, count // core)
    dims = (count // (core * z), z, core)
    half = rank // 2
    lines = 3 * half
    piece = lines // n_blk
    rounds = depth // 2
    chunk = points // count
    lot = rank // 128 * chunk + chunk // 2
    strip = min(128, points // 4)
    vm = lambda *shape: pltpu.VMEM(shape, f32)
    vb = lambda *shape: pltpu.VMEM(shape, bf16)
    dma = lambda *shape: pltpu.SemaphoreType.DMA(shape)
    return pl.pallas_call(
        functools.partial(near_kernel, dims),
        out_shape=(jax.ShapeDtypeStruct((depth + 1, lines, half), f32), jax.ShapeDtypeStruct((points, rank), f32)),
        in_specs=[pl.BlockSpec(memory_space=pltpu.VMEM)] * 2 + [pl.BlockSpec(memory_space=pl.ANY)] * 2,
        out_specs=[pl.BlockSpec(memory_space=pltpu.VMEM)] * 2,
        scratch_shapes=[
            vb(points, points), vb(points, points),
            vm(count, lot, 128), vm(points // strip, 1, strip), vm(count, chunk, rank),
            vm(count, lot, 128), vm(count, 1, strip), vm(count, chunk, rank),
            vm(3, count, lot, 128), vm(points, rank), vb(points, 256), vm(rank, rank),
            vb(points, rank), vb(points, rank),
            vm(lines, half), vm(n_blk - 1, piece, half), vm(rounds, piece, half), vm(rounds, 3, piece, half),
            vm(depth + 1, piece, half), vm(depth + 1, lines, half),
            vm(rank, points), vm(rank, points), dma(2), dma(3), dma(3, 4), dma(4, 4), dma(4, 4),
            dma(n_blk - 1), dma(n_blk - 1), dma(rounds, 3), dma(rounds, 3),
            dma(rounds + 1, n_blk - 1), dma(rounds + 1, n_blk - 1),
        ],
        compiler_params=pltpu.CompilerParams(collective_id=0, has_side_effects=True, vmem_limit_bytes=56 << 20),
    )(slot[None], features, sketch, omega)


def per_device(features, sketch, omega, slot, column_order):
    depth = column_order.shape[0]
    sums, turned = near_field(slot, features, sketch, omega, depth)
    second = lax.axis_index("leaf") >> jnp.arange(depth, dtype=jnp.int32) & 1
    leaf_basis, transfers = tri(column_order, sums, second, turned)
    return (leaf_basis, transfers[None])


def solution(mesh):
    placed = (
        P(None, ("leaf", "blk")),
        P(None, ("leaf", "blk")),
        P(None, ("leaf", "blk")),
        P(("leaf", "blk")),
        P(),
    )
    return jax.shard_map(
        per_device,
        mesh=mesh,
        in_specs=placed,
        out_specs=(P(None, ("leaf", "blk")), P("leaf", None, None, None)),
        check_vma=False,
    )
```
